256 devices in a mesh: gx: 16 (over y_hi, z), gy: 16 (over x, y_lo, core).
Axes of the slice: x: 4, y: 4 (y_hi: 2, y_lo: 2; y = y_hi * 2 + y_lo), z: 8, core: 2. Of those that a mesh axis runs over, the one named last changes fastest.
Arguments:
- fine_solution: float32 [512, 512, 512], P('gx', 'gy'), may hold values from -6 to 6
- fine_source: float32 [512, 512, 512], P('gx', 'gy'), may hold values from -6 to 6
- fine_coef: float32 [512, 512, 512], P('gx', 'gy'), may hold values from 0.25 to 4
- coarse_correction: float32 [256, 256, 256], P('gx', 'gy'), may hold values from -6 to 6
- coarse_source: float32 [256, 256, 256], P('gx', 'gy'), may hold values from -6 to 6
- coarse_coef: float32 [256, 256, 256], P('gx', 'gy'), may hold values from 0.25 to 4
Outputs:
- fine_next: float32 [512, 512, 512], P('gx', 'gy')
- restricted: float32 [256, 256, 256], P('gx', 'gy')
- coarse_next: float32 [256, 256, 256], P('gx', 'gy')
The draws below stay inside these ranges and needn't reach their ends.
All inputs are finite; a program needn't handle non-finite values.
Results may differ from the reference program's by a relative error of at most 0.00015.
Values sent between devices are 32-bit elements; how exact they have to be, the bound alone decides.
No kernel may reach another device: no remote copies, remote signals or barrier semaphores. Data moves between devices by JAX's collectives and lax.ppermute only.
A program may use at most 128 MiB of HBM per device.

```python
import math
import jax
import jax.numpy as jnp

NZ = 512
FINE_STEPS = 4
COARSE_STEPS = 4
NX = 512
NY = 512
MX = 256
MY = 256
MZ = 256


def levels(own_key, shape, pieces, smallest, largest):
    def one(axis_at, blocks):
        heights = jax.random.uniform(jax.random.fold_in(jax.random.fold_in(own_key, 6), axis_at), (blocks,), jnp.float32, smallest / len(pieces), largest / len(pieces))
        return jnp.repeat(jnp.exp(heights), shape[axis_at] // blocks).reshape((-1,) + (1,) * (len(shape) - axis_at - 1))

    loudness = one(*pieces[0])
    for cut in pieces[1:]:
        loudness = loudness * one(*cut)
    return loudness


def gaussian(own_key, shape, spread, reach, cuts=(), held_as=jnp.bfloat16):
    values = jax.random.normal(own_key, shape, jnp.float32) * spread
    if len(cuts) > 0:
        values = levels(own_key, shape, cuts, -0.22, 0.18) * values
    return jnp.clip(values, min=-reach, max=reach).astype(held_as)


def setup_inputs(seed: int = 0) -> dict:
    keys = jax.random.split(jax.random.key(seed), 7)
    fine_solution = gaussian(keys[0], (NX, NY, NZ), 1.0, 6.0, ((0, 16), (1, 16)), jnp.float32)
    fine_source = gaussian(keys[1], (NX, NY, NZ), 1.0, 6.0, ((0, 16), (1, 16)), jnp.float32)
    fine_coef = jnp.clip(jnp.exp(math.log(4.0) - 2.7725887 * jax.random.uniform(keys[2], (NX, NY, NZ), jnp.float32) ** levels(keys[2], (NX, NY, NZ), ((0, 16), (1, 16)), -0.2, 0.2)), 0.25, 4.0)
    coarse_correction = gaussian(keys[3], (MX, MY, MZ), 1.0, 6.0, ((0, 16), (1, 16)), jnp.float32)
    coarse_source = gaussian(keys[4], (MX, MY, MZ), 1.0, 6.0, ((0, 16), (1, 16)), jnp.float32)
    coarse_coef = jnp.clip(jnp.exp(math.log(4.0) - 2.7725887 * jax.random.uniform(keys[5], (MX, MY, MZ), jnp.float32) ** levels(keys[5], (MX, MY, MZ), ((0, 16), (1, 16)), -0.2, 0.2)), 0.25, 4.0)
    return {"fine_solution": fine_solution, "fine_source": fine_source, "fine_coef": fine_coef, "coarse_correction": coarse_correction, "coarse_source": coarse_source, "coarse_coef": coarse_coef}


MASS = 0.2
THETA = 1.125
DELTA = 0.875
SIGMA = THETA / DELTA


def operate(field, coefficient, grid_scale):
    flux_sum = jnp.zeros_like(field)
    face_sum = jnp.zeros_like(field)
    for axis_no in range(3):
        for offset in (1, -1):
            neighbour = jnp.roll(field, offset, axis_no)
            face_coef = 0.5 * (coefficient + jnp.roll(coefficient, offset, axis_no))
            flux_sum = flux_sum + face_coef * (neighbour - field)
            face_sum = face_sum + face_coef
    return MASS * field - grid_scale * flux_sum, MASS + grid_scale * face_sum


def smooth_whole(solution, source, coefficient, grid_scale, sweeps):
    applied, diagonal = operate(solution, coefficient, grid_scale)
    residual = source - applied
    scaled = residual / diagonal
    direction = scaled / THETA
    ratio = 1.0 / SIGMA
    for sweep in range(sweeps):
        solution = solution + direction
        if sweep + 1 < sweeps:
            image, unused = operate(direction, coefficient, grid_scale)
            scaled = scaled - image / diagonal
            next_ratio = 1.0 / (2.0 * SIGMA - ratio)
            direction = next_ratio * ratio * direction + (2.0 * next_ratio / DELTA) * scaled
            ratio = next_ratio
    return solution, residual


def restrict_whole(field, axis_no):
    moved = jnp.moveaxis(field, axis_no, 0)
    even_part = moved[0::2]
    odd_part = moved[1::2]
    result = 0.5 * even_part + 0.25 * (odd_part + jnp.roll(odd_part, 1, 0))
    return jnp.moveaxis(result, 0, axis_no)


def prolong_whole(field, axis_no):
    moved = jnp.moveaxis(field, axis_no, 0)
    odd_part = 0.5 * (moved + jnp.roll(moved, -1, 0))
    joined = jnp.stack([moved, odd_part], 1)
    joined = joined.reshape((2 * moved.shape[0],) + moved.shape[1:])
    return jnp.moveaxis(joined, 0, axis_no)


def reference(fine_solution, fine_source, fine_coef, coarse_correction, coarse_source, coarse_coef):
    smoothed, residual = smooth_whole(fine_solution, fine_source, fine_coef, 1.0, FINE_STEPS)
    restricted = residual
    for axis_no in range(3):
        restricted = restrict_whole(restricted, axis_no)
    lifted = coarse_correction
    for axis_no in range(3):
        lifted = prolong_whole(lifted, axis_no)
    fine_next = smoothed + lifted
    coarse_next, unused = smooth_whole(coarse_correction, coarse_source, coarse_coef, 0.25, COARSE_STEPS)
    return fine_next, restricted, coarse_next
```

```python
import functools

import jax
import jax.numpy as jnp
from jax import lax
from jax.experimental import pallas as pl
from jax.experimental.pallas import tpu as pltpu
from jax.sharding import PartitionSpec as P

MASS = 0.2
THETA = 1.125
DELTA = 0.875
SIGMA = THETA / DELTA
STEPS = 4
F32 = jnp.float32

NF, ZF, TF = 32, 512, 5
NC, ZC, TC = 16, 256, 3
XROWS = 11 * NF + 11 * 8
YROWS = 8 * (NF + NF // 2 + 12)
LIMIT = 56 * 1024 * 1024


def step_factors():
    ratio = 1.0 / SIGMA
    factors = []
    for _ in range(STEPS - 1):
        following = 1.0 / (2.0 * SIGMA - ratio)
        factors.append((following * ratio, 2.0 * following / DELTA))
        ratio = following
    return factors


def upper_rows(shape):
    return lax.broadcasted_iota(jnp.int32, shape, len(shape) - 2) < 4


def turn(block):
    return pltpu.roll(block, 4, axis=block.ndim - 2)


def pair_up(first, second):
    return jnp.where(upper_rows(first.shape), first, turn(second))


def pair_down(first, second):
    return jnp.where(upper_rows(first.shape), turn(second), first)


def halo_first(up, down):
    return jnp.where(upper_rows(up.shape), up, down)


def halo_second(up, down):
    return turn(jnp.where(upper_rows(up.shape), down, up))


def pack_kernel(
    u_lo, u_hi, c_lo, c_hi, f_lo, f_hi,
    u_r0, u_r3, c_r0, c_r3, f_r0, f_r3,
    e, cc, cs, x_lo, x_hi, y_up, y_dn,
):
    k = 0
    for lo, hi, coarse, count in ((u_lo, u_hi, e, 4), (c_lo, c_hi, cc, 4), (f_lo, f_hi, cs, 3)):
        for j in range(count):
            dist = count - 1 - j
            x_lo[NF * k : NF * (k + 1), :] = lo[dist]
            x_hi[NF * k : NF * (k + 1), :] = hi[3 - dist]
            row = 11 * NF + 8 * k
            for half in range(2):
                lanes = slice(ZC * half, ZC * (half + 1))
                rows = slice(8 * half, 8 * (half + 1))
                x_lo[row : row + 8, lanes] = coarse[dist, rows, :]
                x_hi[row : row + 8, lanes] = coarse[NC - 1 - dist, rows, :]
            k += 1

    for x in range(NF):
        y_up[8 * x : 8 * x + 8, :] = pair_up(u_r0[x], c_r0[x])
        y_dn[8 * x : 8 * x + 8, :] = pair_down(u_r3[x], c_r3[x])
    for m in range(NF // 2):
        row = 8 * (NF + m)
        y_up[row : row + 8, :] = pair_up(f_r0[2 * m], f_r0[2 * m + 1])
        y_dn[row : row + 8, :] = pair_down(f_r3[2 * m], f_r3[2 * m + 1])
    for h in range(NC + NC // 2):
        row = 8 * (NF + NF // 2 + h // 2)
        lanes = slice(ZC * (h % 2), ZC * (h % 2 + 1))
        if h < NC:
            pair = ((e, h), (cc, h))
        else:
            pair = ((cs, 2 * (h - NC)), (cs, 2 * (h - NC) + 1))
        low = [ref[i, 0:8, :] for ref, i in pair]
        high = [ref[i, 8:16, :] for ref, i in pair]
        y_up[row : row + 8, lanes] = pair_up(*low)
        y_dn[row : row + 8, lanes] = pair_down(*high)


def pack(u, c, f, e, cc, cs):
    def face(side):
        return pl.BlockSpec((4, NF, ZF), lambda i: (7 * side, 0, 0))

    def strip(at):
        return pl.BlockSpec((NF, 8, ZF), lambda i: (0, at, 0))

    whole = pl.BlockSpec((NC, NC, ZC), lambda i: (0, 0, 0))
    x_spec = pl.BlockSpec((XROWS, ZF), lambda i: (0, 0))
    y_spec = pl.BlockSpec((YROWS, ZF), lambda i: (0, 0))
    return pl.pallas_call(
        pack_kernel,
        grid=(1,),
        in_specs=[face(0), face(1)] * 3 + [strip(0), strip(3)] * 3 + [whole] * 3,
        out_specs=[x_spec, x_spec, y_spec, y_spec],
        out_shape=[jax.ShapeDtypeStruct((XROWS, ZF), F32)] * 2
        + [jax.ShapeDtypeStruct((YROWS, ZF), F32)] * 2,
        compiler_params=pltpu.CompilerParams(vmem_limit_bytes=LIMIT),
        name="pack_faces",
    )(u, u, c, c, f, f, u, u, c, c, f, f, e, cc, cs)


class Slab:
    def __init__(self, planes, tiles, depth, scale, refs):
        self.n, self.t, self.z, self.scale = planes, tiles, depth, scale
        self.lanes = depth // 128
        (
            self.u, self.c, self.f, self.p, self.q, self.total,
            self.wx, self.wy, self.wz, self.inv, self.flux, self.plane,
        ) = refs

    @staticmethod
    def scratch(planes, tiles, depth):
        rows, lanes = 8 * tiles, depth // 128
        split = pltpu.VMEM((planes, lanes, rows, 128), F32)
        whole = pltpu.VMEM((planes, rows, depth), F32)
        return [split] * 3 + [whole] * 7 + [
            pltpu.VMEM((rows, depth), F32),
            pltpu.VMEM((lanes, rows, 128), F32),
        ]

    def tile(self, ref, x, t):
        parts = [ref[x, j, pl.ds(t, 8, stride=self.t), :] for j in range(self.lanes)]
        return jnp.concatenate(parts, axis=1)

    def tiles(self, ref, x):
        return [self.tile(ref, x, t) for t in range(self.t)]

    def rows(self, t):
        return slice(8 * t, 8 * t + 8)

    def put_halo(self, ref, x, block):
        top = 8 * (self.t - 1)
        for j in range(self.lanes):
            ref[x, j, top : top + 8, :] = block[:, 128 * j : 128 * (j + 1)]

    def put_own(self, ref, x, block):
        own = 8 * (self.t - 1)
        for j in range(self.lanes):
            ref[x, j, 0:own, :] = block[:, 128 * j : 128 * (j + 1)]

    def next_row(self, values):
        return values[1:] + [pltpu.roll(values[0], 7, axis=0)]

    def last_row(self, values):
        return [pltpu.roll(values[-1], 1, axis=0)] + values[:-1]

    def next_deep(self, value):
        return pltpu.roll(value, self.z - 1, axis=1)

    def last_deep(self, value):
        return pltpu.roll(value, 1, axis=1)

    def first_pass(self):
        half = 0.5 * self.scale
        u0, u1 = self.tiles(self.u, 0), self.tiles(self.u, 1)
        c0, c1 = self.tiles(self.c, 0), self.tiles(self.c, 1)
        for t in range(self.t):
            w = half * (c0[t] + c1[t])
            self.wx[0, self.rows(t), :] = w
            self.flux[self.rows(t), :] = w * (u1[t] - u0[t])

        def body(x, carry):
            u, c = self.tiles(self.u, x), self.tiles(self.c, x)
            u_row, c_row = self.next_row(u), self.next_row(c)
            wy = [half * (c[t] + c_row[t]) for t in range(self.t)]
            fy = [wy[t] * (u_row[t] - u[t]) for t in range(self.t)]
            wy_last, fy_last = self.last_row(wy), self.last_row(fy)
            for t in range(self.t):
                rows = self.rows(t)
                wx = half * (c[t] + self.tile(self.c, x + 1, t))
                wz = half * (c[t] + self.next_deep(c[t]))
                fx = wx * (self.tile(self.u, x + 1, t) - u[t])
                fz = wz * (self.next_deep(u[t]) - u[t])
                faces = (wx + self.wx[x - 1, rows, :]) + (wy[t] + wy_last[t])
                faces = faces + (wz + self.last_deep(wz))
                inv = 1.0 / (MASS + faces)
                flow = (fx - self.flux[rows, :]) + (fy[t] - fy_last[t])
                flow = flow + (fz - self.last_deep(fz))
                residual = self.tile(self.f, x, t) - MASS * u[t] + flow
                q = residual * inv
                p = q * (1.0 / THETA)
                self.flux[rows, :] = fx
                self.wx[x, rows, :] = wx
                self.wy[x, rows, :] = wy[t]
                self.wz[x, rows, :] = wz
                self.inv[x, rows, :] = inv
                self.q[x, rows, :] = q
                self.p[x, rows, :] = p
                self.total[x, rows, :] = u[t] + p
                for j in range(self.lanes):
                    at = pl.ds(t, 8, stride=self.t)
                    self.f[x, j, at, :] = residual[:, 128 * j : 128 * (j + 1)]
            return carry

        lax.fori_loop(1, self.n - 1, body, 0)

    def step(self, level, emit=None):
        keep, gain = step_factors()[level - 1]
        for t in range(self.t):
            rows = self.rows(t)
            change = self.p[level + 1, rows, :] - self.p[level, rows, :]
            self.flux[rows, :] = self.wx[level, rows, :] * change

        def body(x, carry):
            p = [self.p[x, self.rows(t), :] for t in range(self.t)]
            p_row = self.next_row(p)
            fy = [self.wy[x, self.rows(t), :] * (p_row[t] - p[t]) for t in range(self.t)]
            fy_last = self.last_row(fy)
            for t in range(self.t):
                rows = self.rows(t)
                fx = self.wx[x, rows, :] * (self.p[x + 1, rows, :] - p[t])
                fz = self.wz[x, rows, :] * (self.next_deep(p[t]) - p[t])
                flow = (fx - self.flux[rows, :]) + (fy[t] - fy_last[t])
                flow = flow + (fz - self.last_deep(fz))
                self.flux[rows, :] = fx
                q = self.q[x, rows, :] + self.inv[x, rows, :] * (flow - MASS * p[t])
                new = keep * p[t] + gain * q
                total = self.total[x, rows, :] + new
                if emit is None:
                    self.q[x, rows, :] = q
                    self.p[x, rows, :] = new
                    self.total[x, rows, :] = total
                else:
                    for j in range(self.lanes):
                        at = pl.ds(t, 8, stride=self.t)
                        self.plane[j, at, :] = total[:, 128 * j : 128 * (j + 1)]
            if emit is not None:
                own = 8 * (self.t - 1)
                parts = [self.plane[j, 0:own, :] for j in range(self.lanes)]
                emit(x, jnp.concatenate(parts, axis=1))
            return carry

        lax.fori_loop(1 + level, self.n - 1 - level, body, 0)

    def smooth(self, emit):
        self.first_pass()
        for level in range(1, STEPS):
            self.step(level, emit if level == STEPS - 1 else None)


def depth_table(coarse_axis, shape):
    fine_len = shape[1 - coarse_axis]
    fine = lax.broadcasted_iota(jnp.int32, shape, 1 - coarse_axis)
    coarse = lax.broadcasted_iota(jnp.int32, shape, coarse_axis)
    near = (fine == 2 * coarse + 1) | (fine == lax.rem(2 * coarse - 1 + fine_len, fine_len))
    return jnp.where(fine == 2 * coarse, 1.0, jnp.where(near, 0.5, 0.0))


def exact_dot(field, table):
    table = table.astype(jnp.bfloat16)
    head = field.astype(jnp.bfloat16)
    rest = field - head.astype(F32)
    middle = rest.astype(jnp.bfloat16)
    tail = (rest - middle.astype(F32)).astype(jnp.bfloat16)
    parts = [jnp.dot(v, table, preferred_element_type=F32) for v in (head, middle, tail)]
    return (parts[2] + parts[1]) + parts[0]


def restrict_plane(slab, at, before, after, grown, out_ref, row):
    for j in range(4):
        mixed = 0.5 * slab.f[at, j] + 0.25 * (slab.f[before, j] + slab.f[after, j])
        grown[j, 0:8, :] = mixed[NF : NF + 8]
        grown[j, 8 : 8 + NF, :] = mixed[0:NF]
        middle = grown[j, pl.ds(8, NC, stride=2), :]
        beside = grown[j, pl.ds(9, NC, stride=2), :] + grown[j, pl.ds(7, NC, stride=2), :]
        out_ref[pl.ds(row, NC), 128 * j : 128 * (j + 1)] = 0.5 * middle + 0.25 * beside


def lift_plane(deep, row, lifted, at):
    if not isinstance(row, int):
        row = pl.multiple_of(row, 8)
    block = deep[pl.ds(row, 24), :]
    here, there = block[0:NC], pltpu.roll(block, 23, axis=0)[0:NC]
    between = 0.5 * (here + there)
    for j in range(4):
        lanes = slice(128 * j, 128 * (j + 1))
        lifted[at, j, pl.ds(0, NC, stride=2), :] = here[:, lanes]
        lifted[at, j, pl.ds(1, NC, stride=2), :] = between[:, lanes]


def lifted_plane(lifted, low, high):
    parts = [0.5 * (lifted[low, j] + lifted[high, j]) for j in range(4)]
    return jnp.concatenate(parts, axis=1)


def coarse_halo(y_up, y_dn, base, h):
    row = base + 8 * (h // 2)
    lanes = slice(ZC * (h % 2), ZC * (h % 2 + 1))
    return y_up[row : row + 8, lanes], y_dn[row : row + 8, lanes]


def inner_kernel(u, c, f, e, y_up, y_dn, out, out_r, *scratch):
    sems, grown, mixed, deep, lifted = scratch[:5]
    slab = Slab(NF, TF, ZF, 1.0, scratch[5:])
    copies = []
    for a, (source, target) in enumerate(((u, slab.u), (c, slab.c), (f, slab.f))):
        for j in range(4):
            copies.append(
                pltpu.make_async_copy(
                    source.at[:, :, pl.ds(128 * j, 128)],
                    target.at[:, j, pl.ds(0, NF), :],
                    sems.at[a, j],
                )
            )
    for copy in copies:
        copy.start()

    pieces = []
    for i in range(NC):
        up, down = coarse_halo(y_up, y_dn, 8 * (NF + NF // 2), i)
        pieces += [e[i], halo_first(up, down)]
    deep[...] = exact_dot(jnp.concatenate(pieces, 0), depth_table(0, (ZC, ZF)))

    def raise_one(i, carry):
        lift_plane(deep, 24 * i, lifted, i)
        return carry

    lax.fori_loop(2, NC - 1, raise_one, 0)
    for copy in copies:
        copy.wait()

    def fill(m, carry):
        for half in range(2):
            x = 2 * m + half
            row = pl.multiple_of(8 * x, 8)
            up, down = y_up[pl.ds(row, 8), :], y_dn[pl.ds(row, 8), :]
            slab.put_halo(slab.u, x, halo_first(up, down))
            slab.put_halo(slab.c, x, halo_second(up, down))
        row = pl.multiple_of(8 * (NF + m), 8)
        up, down = y_up[pl.ds(row, 8), :], y_dn[pl.ds(row, 8), :]
        slab.put_halo(slab.f, 2 * m, halo_first(up, down))
        slab.put_halo(slab.f, 2 * m + 1, halo_second(up, down))
        return carry

    lax.fori_loop(0, NF // 2, fill, 0)

    def emit(x, own):
        out[x] = own + lifted_plane(lifted, lax.div(x, 2), lax.div(x + 1, 2))

    slab.smooth(emit)

    def lower(i, carry):
        row = pl.multiple_of(NC * (i - 1), 8)
        restrict_plane(slab, 2 * i, 2 * i - 1, 2 * i + 1, grown, mixed, row)
        return carry

    lax.fori_loop(1, NC - 1, lower, 0)
    result = exact_dot(mixed[...], 0.5 * depth_table(1, (ZF, ZC)))
    for i in range(1, NC - 1):
        out_r[i] = result[NC * (i - 1) : NC * i]


def inner(u, c, f, e, y_up, y_dn):
    anywhere = pl.BlockSpec(memory_space=pl.ANY)
    vmem = pl.BlockSpec(memory_space=pltpu.VMEM)
    return pl.pallas_call(
        inner_kernel,
        in_specs=[anywhere] * 3 + [vmem] * 3,
        out_specs=[vmem, vmem],
        out_shape=[
            jax.ShapeDtypeStruct((NF, NF, ZF), F32),
            jax.ShapeDtypeStruct((NC, NC, ZC), F32),
        ],
        scratch_shapes=[
            pltpu.SemaphoreType.DMA((3, 4)),
            pltpu.VMEM((4, NF + 8, 128), F32),
            pltpu.VMEM((NC * (NC - 2), ZF), F32),
            pltpu.VMEM((24 * NC, ZF), F32),
            pltpu.VMEM((NC, 4, NF, 128), F32),
        ]
        + Slab.scratch(NF, TF, ZF),
        compiler_params=pltpu.CompilerParams(vmem_limit_bytes=LIMIT),
        cost_estimate=pl.CostEstimate(
            flops=30_000_000_000, bytes_accessed=12_000_000, transcendentals=0
        ),
        name="inner_planes",
    )(u, c, f, e, y_up, y_dn)


WIDE = 12


def outer_kernel(
    u, c, f, e, cc, cs, y_up, y_dn, x_lo, x_hi, k_lo, k_hi, mid, mid_r,
    out, out_r, out_c, *scratch,
):
    sems, out_sems, grown, mixed, deep, lifted, edge, edge_r = scratch[:8]
    slabs = [Slab(WIDE, TF, ZF, 1.0, scratch[8 + 12 * i : 20 + 12 * i]) for i in range(2)]
    coarse = Slab(NC + 8, TC, ZC, 0.25, scratch[32:44])
    copies = [[], []]
    for side in range(2):
        slab = slabs[side]
        for a, (source, target) in enumerate(((u, slab.u), (c, slab.c), (f, slab.f))):
            for j in range(4):
                copies[side].append(
                    pltpu.make_async_copy(
                        source.at[pl.ds(24 * side, 8), :, pl.ds(128 * j, 128)],
                        target.at[pl.ds(4 * (1 - side), 8), j, pl.ds(0, NF), :],
                        sems.at[side, a, j],
                    )
                )
    for copy in copies[0] + copies[1]:
        copy.start()

    base = 8 * (NF + NF // 2)
    for x in range(NC):
        for target, source in ((coarse.u, e), (coarse.c, cc), (coarse.f, cs)):
            coarse.put_own(target, x + 4, source[x])
        pair = coarse_halo(y_up, y_dn, base, x)
        coarse.put_halo(coarse.u, x + 4, halo_first(*pair))
        coarse.put_halo(coarse.c, x + 4, halo_second(*pair))
        pair = coarse_halo(y_up, y_dn, base, NC + x // 2)
        choose = halo_second if x % 2 else halo_first
        coarse.put_halo(coarse.f, x + 4, choose(*pair))
    for side, faces, corner in ((0, x_lo, k_lo), (1, x_hi, k_hi)):
        slab = slabs[side]
        k = 0
        for which, count in ((0, 4), (1, 4), (2, 3)):
            fine_ref = (slab.u, slab.c, slab.f)[which]
            coarse_ref = (coarse.u, coarse.c, coarse.f)[which]
            for m in range(count):
                dist = count - m
                at = 4 - dist if side == 0 else 7 + dist
                fine_ref_rows = faces[NF * k : NF * (k + 1), :]
                slab.put_own(fine_ref, at, fine_ref_rows)
                row = 11 * NF + 8 * k
                at_c = 4 - dist if side == 0 else 3 + NC + dist
                halves = [faces[row : row + 8, ZC * h : ZC * (h + 1)] for h in range(2)]
                coarse.put_own(coarse_ref, at_c, jnp.concatenate(halves, 0))
                k += 1
                if dist == 4 or (which == 2 and dist == 3):
                    fine_ref[at, :, NF : NF + 8, :] = jnp.zeros((4, 8, 128), F32)
                    coarse_ref[at_c, :, NC : NC + 8, :] = jnp.zeros((2, 8, 128), F32)
                    continue
                if which < 2:
                    near = dist - 1 if side == 1 else 3 - dist
                    up, down = 8 * near, 8 * (3 + near)
                    choose = halo_first if which == 0 else halo_second
                    h = dist - 1 if side == 1 else 4 - dist
                    up_c, down_c = 64 + 8 * (h // 2), 88 + 8 * (h // 2)
                    lanes_c = slice(ZC * (h % 2), ZC * (h % 2 + 1))
                else:
                    plane = dist - 1 if side == 1 else 2 - dist
                    up, down = 48, 56
                    choose = halo_second if plane else halo_first
                    up_c, down_c = 80, 104
                    half = 0 if side == 1 else 1
                    lanes_c = slice(ZC * half, ZC * (half + 1))
                block = choose(corner[up : up + 8, :], corner[down : down + 8, :])
                slab.put_halo(fine_ref, at, block)
                block = choose(corner[up_c : up_c + 8, lanes_c], corner[down_c : down_c + 8, lanes_c])
                coarse.put_halo(coarse_ref, at_c, block)

    pieces = []
    for x in (0, 1, 2, 14, 15, 16):
        pieces.append(jnp.concatenate([coarse.u[x + 4, j] for j in range(2)], axis=1))
    deep[...] = exact_dot(jnp.concatenate(pieces, 0), depth_table(0, (ZC, ZF)))
    for i in range(6):
        lift_plane(deep, 24 * i, lifted, i)

    def emit_coarse(x, own):
        out_c[x - 4] = own

    coarse.smooth(emit_coarse)

    finish = []
    for side in range(2):
        slab = slabs[side]
        for copy in copies[side]:
            copy.wait()
        for i in range(8):
            x = 24 * side + i
            at = i + 4 * (1 - side)
            pair = (y_up[8 * x : 8 * x + 8, :], y_dn[8 * x : 8 * x + 8, :])
            slab.put_halo(slab.u, at, halo_first(*pair))
            slab.put_halo(slab.c, at, halo_second(*pair))
            row = 8 * (NF + x // 2)
            pair = (y_up[row : row + 8, :], y_dn[row : row + 8, :])
            slab.put_halo(slab.f, at, (halo_second if x % 2 else halo_first)(*pair))

        def emit(x, own, side=side):
            low = 3 * side + lax.div(x - 4, 2)
            high = 3 * side + lax.div(x - 3, 2)
            edge[side, x - 4] = own + lifted_plane(lifted, low, high)

        slab.smooth(emit)
        at = 4 if side == 0 else 6
        restrict_plane(slab, at, at - 1, at + 1, grown, mixed, NC * side)
        finish.append(
            pltpu.make_async_copy(
                edge.at[side], out.at[pl.ds((NF - 4) * side, 4)], out_sems.at[side]
            )
        )
        finish[-1].start()

    result = exact_dot(mixed[...], 0.5 * depth_table(1, (ZF, ZC)))
    for side in range(2):
        edge_r[side, 0] = result[NC * side : NC * (side + 1)]
        finish.append(
            pltpu.make_async_copy(
                edge_r.at[side], out_r.at[pl.ds((NC - 1) * side, 1)], out_sems.at[2 + side]
            )
        )
        finish[-1].start()
    for copy in finish:
        copy.wait()


def outer(u, c, f, e, cc, cs, y_up, y_dn, x_lo, x_hi, k_lo, k_hi, mid, mid_r):
    anywhere = pl.BlockSpec(memory_space=pl.ANY)
    vmem = pl.BlockSpec(memory_space=pltpu.VMEM)
    return pl.pallas_call(
        outer_kernel,
        in_specs=[anywhere] * 3 + [vmem] * 9 + [anywhere] * 2,
        out_specs=[anywhere, anywhere, vmem],
        out_shape=[
            jax.ShapeDtypeStruct((NF, NF, ZF), F32),
            jax.ShapeDtypeStruct((NC, NC, ZC), F32),
            jax.ShapeDtypeStruct((NC, NC, ZC), F32),
        ],
        scratch_shapes=[
            pltpu.SemaphoreType.DMA((2, 3, 4)),
            pltpu.SemaphoreType.DMA((4,)),
            pltpu.VMEM((4, NF + 8, 128), F32),
            pltpu.VMEM((2 * NC, ZF), F32),
            pltpu.VMEM((24 * 6, ZF), F32),
            pltpu.VMEM((6, 4, NF, 128), F32),
            pltpu.VMEM((2, 4, NF, ZF), F32),
            pltpu.VMEM((2, 1, NC, ZC), F32),
        ]
        + Slab.scratch(WIDE, TF, ZF) * 2
        + Slab.scratch(NC + 8, TC, ZC),
        compiler_params=pltpu.CompilerParams(vmem_limit_bytes=LIMIT),
        input_output_aliases={12: 0, 13: 1},
        name="outer_planes",
    )(u, c, f, e, cc, cs, y_up, y_dn, x_lo, x_hi, k_lo, k_hi, mid, mid_r)


def shift(block, axis, by):
    count = lax.axis_size(axis)
    return lax.ppermute(block, axis, [(i, (i + by) % count) for i in range(count)])


def relay(y_up, y_dn, side):
    spans = (((0, 3), (32, 33), (48, 50), (56, 57)), ((29, 32), (47, 48), (54, 56), (59, 60)))[side]
    pieces = []
    for group in ((0,), (1,), (2, 3)):
        for ref in (y_up, y_dn):
            for member in group:
                a, b = spans[member]
                pieces.append(ref[8 * a : 8 * b])
    return jnp.concatenate(pieces, 0)


def local(u, f, c, e, cs, cc):
    x_lo, x_hi, y_up, y_dn = pack(u, c, f, e, cc, cs)
    y_up = shift(y_up, "gy", -1)
    y_dn = shift(y_dn, "gy", 1)
    from_hi = shift(x_lo, "gx", -1)
    from_lo = shift(x_hi, "gx", 1)
    corner_hi = shift(relay(y_up, y_dn, 0), "gx", -1)
    corner_lo = shift(relay(y_up, y_dn, 1), "gx", 1)
    mid, mid_r = inner(u, c, f, e, y_up, y_dn)
    return tuple(
        outer(u, c, f, e, cc, cs, y_up, y_dn, from_lo, from_hi, corner_lo, corner_hi, mid, mid_r)
    )


def solution(mesh):
    placed = P("gx", "gy", None)
    return jax.shard_map(
        local,
        mesh=mesh,
        in_specs=(placed,) * 6,
        out_specs=(placed,) * 3,
        check_vma=False,
    )
```

```python
import jax
import jax.numpy as jnp
from jax import lax
from jax.experimental import pallas as pl
from jax.experimental.pallas import tpu as pltpu
from jax.sharding import PartitionSpec as P

MASS = 0.2
THETA = 1.125
DELTA = 0.875
SIGMA = THETA / DELTA
STEPS = 4
F32 = jnp.float32

NF, ZF, TF = 32, 512, 5
NC, ZC, TC = 16, 256, 3
XROWS = 7 * 8 * TF + 4 * 8 * TC
YROWS = 8 * (NF + NF // 2 + 12)
LIMIT = 56 * 1024 * 1024


def step_factors():
    ratio = 1.0 / SIGMA
    factors = []
    for _ in range(STEPS - 1):
        following = 1.0 / (2.0 * SIGMA - ratio)
        factors.append((following * ratio, 2.0 * following / DELTA))
        ratio = following
    return factors


def upper_rows(shape):
    return lax.broadcasted_iota(jnp.int32, shape, len(shape) - 2) < 4


def turn(block):
    return pltpu.roll(block, 4, axis=block.ndim - 2)


def pair_up(first, second):
    return jnp.where(upper_rows(first.shape), first, turn(second))


def pair_down(first, second):
    return jnp.where(upper_rows(first.shape), turn(second), first)


def halo_first(up, down):
    return jnp.where(upper_rows(up.shape), up, down)


def halo_second(up, down):
    return turn(jnp.where(upper_rows(up.shape), down, up))


def pack_y_kernel(u_r0, u_r3, c_r0, c_r3, f_r0, f_r3, e, cc, cs, y_up, y_dn):
    for x in range(NF):
        y_up[8 * x : 8 * x + 8, :] = pair_up(u_r0[x], c_r0[x])
        y_dn[8 * x : 8 * x + 8, :] = pair_down(u_r3[x], c_r3[x])
    for m in range(NF // 2):
        row = 8 * (NF + m)
        y_up[row : row + 8, :] = pair_up(f_r0[2 * m], f_r0[2 * m + 1])
        y_dn[row : row + 8, :] = pair_down(f_r3[2 * m], f_r3[2 * m + 1])
    for h in range(NC + NC // 2):
        row = 8 * (NF + NF // 2 + h // 2)
        lanes = slice(ZC * (h % 2), ZC * (h % 2 + 1))
        if h < NC:
            pair = ((e, h), (cc, h))
        else:
            pair = ((cs, 2 * (h - NC)), (cs, 2 * (h - NC) + 1))
        low = [ref[i, 0:8, :] for ref, i in pair]
        high = [ref[i, 8:16, :] for ref, i in pair]
        y_up[row : row + 8, lanes] = pair_up(*low)
        y_dn[row : row + 8, lanes] = pair_down(*high)


def pack_y(u, c, f, e, cc, cs):
    def strip(at):
        return pl.BlockSpec((NF, 8, ZF), lambda i: (0, at, 0))

    whole = pl.BlockSpec((NC, NC, ZC), lambda i: (0, 0, 0))
    y_spec = pl.BlockSpec((YROWS, ZF), lambda i: (0, 0))
    return pl.pallas_call(
        pack_y_kernel,
        grid=(1,),
        in_specs=[strip(0), strip(3)] * 3 + [whole] * 3,
        out_specs=[y_spec, y_spec],
        out_shape=[jax.ShapeDtypeStruct((YROWS, ZF), F32)] * 2,
        compiler_params=pltpu.CompilerParams(vmem_limit_bytes=LIMIT),
        name="pack_gy_faces",
    )(u, u, c, c, f, f, e, cc, cs)


class Slab:
    def __init__(self, own, tiles, depth, scale, natural, work, shift=0, flipped=False):
        self.own, self.t, self.z, self.scale = own, tiles, depth, scale
        self.lanes, self.shift, self.flipped = depth // 128, shift, flipped
        self.u, self.c, self.f = natural
        if work:
            (
                self.p, self.q, self.total, self.wx, self.wy, self.wz, self.wz_last,
                self.inv, self.flux, self.plane,
            ) = work

    @staticmethod
    def natural(planes, tiles, depth):
        return [pltpu.VMEM((planes, depth // 128, 8 * tiles, 128), F32)] * 3

    @staticmethod
    def work(planes, tiles, depth):
        rows, lanes = 8 * tiles, depth // 128
        return [pltpu.VMEM((planes, rows, depth), F32)] * 8 + [
            pltpu.VMEM((rows, depth), F32),
            pltpu.VMEM((lanes, rows, 128), F32),
        ]

    def at(self, x):
        return self.own - 1 - (x - self.shift) if self.flipped else x - self.shift

    def tile(self, ref, x, t):
        x = self.at(x)
        parts = [ref[x, j, pl.ds(t, 8, stride=self.t), :] for j in range(self.lanes)]
        return jnp.concatenate(parts, axis=1)

    def tiles(self, ref, x):
        return [self.tile(ref, x, t) for t in range(self.t)]

    def put_tile(self, ref, index, t, value):
        for j in range(self.lanes):
            ref[index, j, pl.ds(t, 8, stride=self.t), :] = value[:, 128 * j : 128 * (j + 1)]

    def rows(self, t):
        return slice(8 * t, 8 * t + 8)

    def put_halo(self, ref, index, block):
        top = 8 * (self.t - 1)
        for j in range(self.lanes):
            ref[index, j, top : top + 8, :] = block[:, 128 * j : 128 * (j + 1)]

    def put_own(self, ref, index, block):
        own = 8 * (self.t - 1)
        for j in range(self.lanes):
            ref[index, j, 0:own, :] = block[:, 128 * j : 128 * (j + 1)]

    def next_row(self, values):
        return values[1:] + [pltpu.roll(values[0], 7, axis=0)]

    def last_row(self, values):
        return [pltpu.roll(values[-1], 1, axis=0)] + values[:-1]

    def next_deep(self, value):
        return pltpu.roll(value, self.z - 1, axis=1)

    def last_deep(self, value):
        return pltpu.roll(value, 1, axis=1)

    def cross_weights(self, c):
        half = 0.5 * self.scale
        ahead, behind = self.next_row(c), self.last_row(c)
        wy = [half * (c[t] + ahead[t]) for t in range(self.t)]
        wy_last = [half * (c[0] + behind[0])] + wy[:-1]
        wz = [half * (v + self.next_deep(v)) for v in c]
        wz_last = [half * (v + self.last_deep(v)) for v in c]
        return wy, wy_last, wz, wz_last

    def cross_flow(self, v, wy, wy_last, wz, wz_last):
        ahead, behind = self.next_row(v), self.last_row(v)
        fy = [wy[t] * (ahead[t] - v[t]) for t in range(self.t)]
        fy_last = [wy_last[0] * (v[0] - behind[0])] + fy[:-1]
        flow = []
        for t in range(self.t):
            fz = wz[t] * (self.next_deep(v[t]) - v[t])
            fz_last = wz_last[t] * (v[t] - self.last_deep(v[t]))
            flow.append((fy[t] - fy_last[t]) + (fz - fz_last))
        return flow

    def keep_weights(self, x, t, wy, wz, wz_last, faces):
        rows = self.rows(t)
        inv = 1.0 / (MASS + faces)
        self.wy[x, rows, :] = wy
        self.wz[x, rows, :] = wz
        self.wz_last[x, rows, :] = wz_last
        self.inv[x, rows, :] = inv
        return inv

    def open_end(self, x):
        u0, u1 = self.tiles(self.u, x), self.tiles(self.u, x + 1)
        c0, c1 = self.tiles(self.c, x), self.tiles(self.c, x + 1)
        for t in range(self.t):
            w = 0.5 * self.scale * (c0[t] + c1[t])
            self.wx[x, self.rows(t), :] = w
            self.flux[self.rows(t), :] = w * (u1[t] - u0[t])

    def halo_end(self, far, read, start):
        half = 0.5 * self.scale
        step = 1 if start else -1
        mid, near, own = far + step, far + 2 * step, far + 3 * step
        message = [[read(k, t) for t in range(self.t)] for k in range(7)]
        u1, c1, c2, c3, r1, p2, p3 = message
        u_own, c_own = self.tiles(self.u, own), self.tiles(self.c, own)
        cross2, cross1 = self.cross_weights(c2), self.cross_weights(c1)
        for t in range(self.t):
            rows = self.rows(t)
            outer, middle, inner = half * (c3[t] + c2[t]), half * (c2[t] + c1[t]), half * (c1[t] + c_own[t])
            self.wx[min(far, mid), rows, :] = outer
            self.wx[min(mid, near), rows, :] = middle
            self.wx[min(near, own), rows, :] = inner
            self.p[far, rows, :] = p3[t]
            wy, wy_last, wz, wz_last = [w[t] for w in cross2]
            faces = (outer + middle) + (wy + wy_last) + (wz + wz_last)
            self.keep_weights(mid, t, wy, wz, wz_last, faces)
            self.p[mid, rows, :] = p2[t]
            self.q[mid, rows, :] = THETA * p2[t]
            wy, wy_last, wz, wz_last = [w[t] for w in cross1]
            faces = (middle + inner) + (wy + wy_last) + (wz + wz_last)
            inv = self.keep_weights(near, t, wy, wz, wz_last, faces)
            flux = inner * (u_own[t] - u1[t])
            residual = r1[t] + flux
            q = residual * inv
            self.q[near, rows, :] = q
            self.p[near, rows, :] = q * (1.0 / THETA)
            if start:
                self.flux[rows, :] = flux
                self.put_tile(self.f, self.own, t, residual)

    def first_plane(self, x):
        half = 0.5 * self.scale
        u, c = self.tiles(self.u, x), self.tiles(self.c, x)
        wy, wy_last, wz, wz_last = self.cross_weights(c)
        cross = self.cross_flow(u, wy, wy_last, wz, wz_last)
        for t in range(self.t):
            rows = self.rows(t)
            wx = half * (c[t] + self.tile(self.c, x + 1, t))
            fx = wx * (self.tile(self.u, x + 1, t) - u[t])
            faces = (wx + self.wx[x - 1, rows, :]) + (wy[t] + wy_last[t]) + (wz[t] + wz_last[t])
            inv = self.keep_weights(x, t, wy[t], wz[t], wz_last[t], faces)
            flow = (fx - self.flux[rows, :]) + cross[t]
            residual = self.tile(self.f, x, t) - MASS * u[t] + flow
            q = residual * inv
            p = q * (1.0 / THETA)
            self.flux[rows, :] = fx
            self.wx[x, rows, :] = wx
            self.q[x, rows, :] = q
            self.p[x, rows, :] = p
            self.total[x, rows, :] = u[t] + p
            self.put_tile(self.f, self.at(x), t, residual)

    def start_step(self, x):
        for t in range(self.t):
            rows = self.rows(t)
            change = self.p[x, rows, :] - self.p[x - 1, rows, :]
            self.flux[rows, :] = self.wx[x - 1, rows, :] * change

    def step_plane(self, level, x, emit):
        keep, gain = step_factors()[level - 1]
        p = [self.p[x, self.rows(t), :] for t in range(self.t)]
        weights = [
            [ref[x, self.rows(t), :] for t in range(self.t)]
            for ref in (self.wy, self.wz, self.wz_last)
        ]
        wy_last = self.last_row(weights[0])
        cross = self.cross_flow(p, weights[0], wy_last, weights[1], weights[2])
        for t in range(self.t):
            rows = self.rows(t)
            fx = self.wx[x, rows, :] * (self.p[x + 1, rows, :] - p[t])
            flow = (fx - self.flux[rows, :]) + cross[t]
            self.flux[rows, :] = fx
            q = self.q[x, rows, :] + self.inv[x, rows, :] * (flow - MASS * p[t])
            new = keep * p[t] + gain * q
            total = self.total[x, rows, :] + new
            if emit is None:
                self.q[x, rows, :] = q
                self.p[x, rows, :] = new
                self.total[x, rows, :] = total
            else:
                for j in range(self.lanes):
                    at = pl.ds(t, 8, stride=self.t)
                    self.plane[j, at, :] = total[:, 128 * j : 128 * (j + 1)]
        if emit is not None:
            own = 8 * (self.t - 1)
            parts = [self.plane[j, 0:own, :] for j in range(self.lanes)]
            emit(x, jnp.concatenate(parts, axis=1))


def sweep(slabs, low, high, act, unroll=2):
    def body(x, carry):
        for slab in slabs:
            act(slab, x)
        return carry

    lax.fori_loop(low, high, body, 0, unroll=unroll)


def smooth(slabs, first, last, low, high, emits, unroll=2):
    sweep(slabs, first, last, lambda slab, x: slab.first_plane(x), unroll)
    for level in range(1, STEPS):
        for slab in slabs:
            slab.start_step(low(level))

        def act(slab, x, level=level):
            emit = emits[slabs.index(slab)] if level == STEPS - 1 else None
            slab.step_plane(level, x, emit)

        sweep(slabs, low(level), high(level), act, unroll)


def depth_table(coarse_axis, shape):
    fine_len = shape[1 - coarse_axis]
    fine = lax.broadcasted_iota(jnp.int32, shape, 1 - coarse_axis)
    coarse = lax.broadcasted_iota(jnp.int32, shape, coarse_axis)
    near = (fine == 2 * coarse + 1) | (fine == lax.rem(2 * coarse - 1 + fine_len, fine_len))
    return jnp.where(fine == 2 * coarse, 1.0, jnp.where(near, 0.5, 0.0))


def exact_dot(field, table):
    table = table.astype(jnp.bfloat16)
    head = field.astype(jnp.bfloat16)
    rest = field - head.astype(F32)
    middle = rest.astype(jnp.bfloat16)
    tail = (rest - middle.astype(F32)).astype(jnp.bfloat16)
    parts = [jnp.dot(v, table, preferred_element_type=F32) for v in (head, middle, tail)]
    return (parts[2] + parts[1]) + parts[0]


def restrict_plane(slab, at, before, after, grown, out_ref, row):
    for j in range(4):
        mixed = 0.5 * slab.f[at, j] + 0.25 * (slab.f[before, j] + slab.f[after, j])
        grown[j, 0:8, :] = mixed[NF : NF + 8]
        grown[j, 8 : 8 + NF, :] = mixed[0:NF]
        middle = grown[j, pl.ds(8, NC, stride=2), :]
        beside = grown[j, pl.ds(9, NC, stride=2), :] + grown[j, pl.ds(7, NC, stride=2), :]
        out_ref[pl.ds(row, NC), 128 * j : 128 * (j + 1)] = 0.5 * middle + 0.25 * beside


def lift_plane(deep, row, lifted, at):
    if not isinstance(row, int):
        row = pl.multiple_of(row, 8)
    block = deep[pl.ds(row, 24), :]
    here, there = block[0:NC], pltpu.roll(block, 23, axis=0)[0:NC]
    between = 0.5 * (here + there)
    for j in range(4):
        lanes = slice(128 * j, 128 * (j + 1))
        lifted[at, j, pl.ds(0, NC, stride=2), :] = here[:, lanes]
        lifted[at, j, pl.ds(1, NC, stride=2), :] = between[:, lanes]


def lifted_plane(lifted, low, high):
    parts = [0.5 * (lifted[low, j] + lifted[high, j]) for j in range(4)]
    return jnp.concatenate(parts, axis=1)


def coarse_halo(y_up, y_dn, base, h):
    row = base + 8 * (h // 2)
    lanes = slice(ZC * (h % 2), ZC * (h % 2 + 1))
    return y_up[row : row + 8, lanes], y_dn[row : row + 8, lanes]


def inner_kernel(u, c, f, e, y_up, y_dn, out, out_r, *scratch):
    sems, grown, mixed, deep, lifted = scratch[:5]
    slab = Slab(NF, TF, ZF, 1.0, scratch[5:8], scratch[8:])
    copies = []
    for a, (source, target) in enumerate(((u, slab.u), (c, slab.c), (f, slab.f))):
        for j in range(4):
            copies.append(
                pltpu.make_async_copy(
                    source.at[:, :, pl.ds(128 * j, 128)],
                    target.at[:, j, pl.ds(0, NF), :],
                    sems.at[a, j],
                )
            )
    for copy in copies:
        copy.start()

    pieces = []
    for i in range(NC):
        up, down = coarse_halo(y_up, y_dn, 8 * (NF + NF // 2), i)
        pieces += [e[i], halo_first(up, down)]
    deep[...] = exact_dot(jnp.concatenate(pieces, 0), depth_table(0, (ZC, ZF)))

    def raise_one(i, carry):
        lift_plane(deep, 24 * i, lifted, i)
        return carry

    lax.fori_loop(2, NC - 1, raise_one, 0)
    for copy in copies:
        copy.wait()

    def fill(m, carry):
        for half in range(2):
            x = 2 * m + half
            row = pl.multiple_of(8 * x, 8)
            up, down = y_up[pl.ds(row, 8), :], y_dn[pl.ds(row, 8), :]
            slab.put_halo(slab.u, x, halo_first(up, down))
            slab.put_halo(slab.c, x, halo_second(up, down))
        row = pl.multiple_of(8 * (NF + m), 8)
        up, down = y_up[pl.ds(row, 8), :], y_dn[pl.ds(row, 8), :]
        slab.put_halo(slab.f, 2 * m, halo_first(up, down))
        slab.put_halo(slab.f, 2 * m + 1, halo_second(up, down))
        return carry

    lax.fori_loop(0, NF // 2, fill, 0)

    def emit(x, own):
        out[x] = own + lifted_plane(lifted, lax.div(x, 2), lax.div(x + 1, 2))

    slab.open_end(0)
    smooth([slab], 1, NF - 1, lambda k: 1 + k, lambda k: NF - 1 - k, [emit])

    def lower(i, carry):
        row = pl.multiple_of(NC * (i - 1), 8)
        restrict_plane(slab, 2 * i, 2 * i - 1, 2 * i + 1, grown, mixed, row)
        return carry

    lax.fori_loop(1, NC - 1, lower, 0)
    result = exact_dot(mixed[...], 0.5 * depth_table(1, (ZF, ZC)))
    for i in range(1, NC - 1):
        out_r[i] = result[NC * (i - 1) : NC * i]


def inner(u, c, f, e, y_up, y_dn):
    anywhere = pl.BlockSpec(memory_space=pl.ANY)
    vmem = pl.BlockSpec(memory_space=pltpu.VMEM)
    return pl.pallas_call(
        inner_kernel,
        in_specs=[anywhere] * 3 + [vmem] * 3,
        out_specs=[vmem, vmem],
        out_shape=[
            jax.ShapeDtypeStruct((NF, NF, ZF), F32),
            jax.ShapeDtypeStruct((NC, NC, ZC), F32),
        ],
        scratch_shapes=[
            pltpu.SemaphoreType.DMA((3, 4)),
            pltpu.VMEM((4, NF + 8, 128), F32),
            pltpu.VMEM((NC * (NC - 2), ZF), F32),
            pltpu.VMEM((24 * NC, ZF), F32),
            pltpu.VMEM((NC, 4, NF, 128), F32),
        ]
        + Slab.natural(NF, TF, ZF)
        + Slab.work(NF, TF, ZF),
        compiler_params=pltpu.CompilerParams(vmem_limit_bytes=LIMIT),
        cost_estimate=pl.CostEstimate(
            flops=30_000_000_000, bytes_accessed=12_000_000, transcendentals=0
        ),
        name="inner_planes",
    )(u, c, f, e, y_up, y_dn)


def first_planes(slab, write):
    half = 0.5 * slab.scale
    u, c = [[slab.tiles(ref, x) for x in range(4)] for ref in (slab.u, slab.c)]
    wx = [[half * (c[x][t] + c[x + 1][t]) for t in range(slab.t)] for x in range(3)]
    fx = [[wx[x][t] * (u[x + 1][t] - u[x][t]) for t in range(slab.t)] for x in range(3)]
    for t in range(slab.t):
        write(0, t, u[0][t])
        for x in range(3):
            write(1 + x, t, c[x][t])
    for x in range(3):
        weights = slab.cross_weights(c[x])
        cross = slab.cross_flow(u[x], *weights)
        for t in range(slab.t):
            part = slab.tile(slab.f, x, t) - MASS * u[x][t] + cross[t] + fx[x][t]
            if x == 0:
                write(4, t, part)
                continue
            wy, wy_last, wz, wz_last = [w[t] for w in weights]
            faces = (wx[x][t] + wx[x - 1][t]) + (wy + wy_last) + (wz + wz_last)
            write(4 + x, t, (part - fx[x - 1][t]) / (MASS + faces) * (1.0 / THETA))


def fine_place(k, t):
    row = 8 * TF * k + 8 * t
    return slice(row, row + 8), slice(0, ZF)


def coarse_place(k, t):
    row = 7 * 8 * TF + 8 * TC * (k // 2) + 8 * t
    return slice(row, row + 8), slice(ZC * (k % 2), ZC * (k % 2 + 1))


def fill_fine(slab, refs, blocks, first, planes):
    y_up, y_dn = refs
    for i in range(planes):
        x = first + i
        if blocks is not None:
            for target, block in zip((slab.u, slab.c, slab.f), blocks):
                slab.put_own(target, i, block[i])
        pair = (y_up[8 * x : 8 * x + 8, :], y_dn[8 * x : 8 * x + 8, :])
        slab.put_halo(slab.u, i, halo_first(*pair))
        slab.put_halo(slab.c, i, halo_second(*pair))
        row = 8 * (NF + x // 2)
        pair = (y_up[row : row + 8, :], y_dn[row : row + 8, :])
        slab.put_halo(slab.f, i, (halo_second if x % 2 else halo_first)(*pair))


def fill_coarse(slab, refs, fields, planes):
    base = 8 * (NF + NF // 2)
    for x, place in planes:
        for target, source in zip((slab.u, slab.c, slab.f), fields):
            slab.put_own(target, place, source[x])
        pair = coarse_halo(*refs, base, x)
        slab.put_halo(slab.u, place, halo_first(*pair))
        slab.put_halo(slab.c, place, halo_second(*pair))
        pair = coarse_halo(*refs, base, NC + x // 2)
        slab.put_halo(slab.f, place, (halo_second if x % 2 else halo_first)(*pair))


def pack_x_kernel(
    u_lo, u_hi, c_lo, c_hi, f_lo, f_hi, e, cc, cs, y_up, y_dn, x_lo, x_hi, *scratch
):
    for side, blocks, out in ((0, (u_lo, c_lo, f_lo), x_lo), (1, (u_hi, c_hi, f_hi), x_hi)):
        slab = Slab(4, TF, ZF, 1.0, scratch[6 * side : 6 * side + 3], (), 0, side == 1)
        fill_fine(slab, (y_up, y_dn), blocks, 28 * side, 4)

        def write_fine(k, t, value, out=out):
            out[fine_place(k, t)] = value

        first_planes(slab, write_fine)
        slab = Slab(4, TC, ZC, 0.25, scratch[6 * side + 3 : 6 * side + 6], (), 0, side == 1)
        fill_coarse(slab, (y_up, y_dn), (e, cc, cs), [(12 * side + i, i) for i in range(4)])

        def write_coarse(k, t, value, out=out):
            out[coarse_place(k, t)] = value

        first_planes(slab, write_coarse)
        for t in range(TC):
            out[coarse_place(7, t)] = jnp.zeros((8, ZC), F32)


def pack_x(u, c, f, e, cc, cs, y_up, y_dn):
    def face(side):
        return pl.BlockSpec((4, NF, ZF), lambda i: (7 * side, 0, 0))

    whole = pl.BlockSpec((NC, NC, ZC), lambda i: (0, 0, 0))
    y_spec = pl.BlockSpec((YROWS, ZF), lambda i: (0, 0))
    x_spec = pl.BlockSpec((XROWS, ZF), lambda i: (0, 0))
    return pl.pallas_call(
        pack_x_kernel,
        grid=(1,),
        in_specs=[face(0), face(1)] * 3 + [whole] * 3 + [y_spec] * 2,
        out_specs=[x_spec, x_spec],
        out_shape=[jax.ShapeDtypeStruct((XROWS, ZF), F32)] * 2,
        scratch_shapes=(Slab.natural(4, TF, ZF) + Slab.natural(4, TC, ZC)) * 2,
        compiler_params=pltpu.CompilerParams(vmem_limit_bytes=LIMIT),
        name="pack_gx_faces",
    )(u, u, c, c, f, f, e, cc, cs, y_up, y_dn)


WIDE = 8


def outer_kernel(
    u, c, f, e, cc, cs, y_up, y_dn, x_lo, x_hi, mid, mid_r, out, out_r, out_c, *scratch
):
    sems, out_sems, grown, mixed, deep, lifted, edge, edge_r = scratch[:8]
    slabs = []
    for side in range(2):
        refs = scratch[8 + 13 * side : 21 + 13 * side]
        slabs.append(Slab(WIDE, TF, ZF, 1.0, refs[:3], refs[3:], 3, side == 1))
    coarse = Slab(NC, TC, ZC, 0.25, scratch[34:37], scratch[37:47], 3)
    copies = []
    for side in range(2):
        slab = slabs[side]
        for a, (source, target) in enumerate(((u, slab.u), (c, slab.c), (f, slab.f))):
            for j in range(4):
                copies.append(
                    pltpu.make_async_copy(
                        source.at[pl.ds((NF - WIDE) * side, WIDE), :, pl.ds(128 * j, 128)],
                        target.at[pl.ds(0, WIDE), j, pl.ds(0, NF), :],
                        sems.at[side, a, j],
                    )
                )
    for copy in copies:
        copy.start()

    fill_coarse(coarse, (y_up, y_dn), (e, cc, cs), [(x, x) for x in range(NC)])
    for t in range(TC):
        coarse.put_tile(coarse.u, NC, t, x_hi[coarse_place(0, t)])
        coarse.put_tile(coarse.c, NC, t, x_hi[coarse_place(1, t)])
    coarse.halo_end(0, lambda k, t: x_lo[coarse_place(k, t)], True)
    sweep([coarse], 3, 3 + NC, lambda slab, x: slab.first_plane(x))
    coarse.halo_end(5 + NC, lambda k, t: x_hi[coarse_place(k, t)], False)
    for level in range(1, STEPS):
        coarse.start_step(level)

        def act(slab, x, level=level):
            def emit(x, own):
                out_c[x - 3] = own

            slab.step_plane(level, x, emit if level == STEPS - 1 else None)

        sweep([coarse], level, 6 + NC - level, act)

    pieces = []
    for x in (0, 1, 2, 14, 15, 16):
        pieces.append(jnp.concatenate([coarse.u[x, j] for j in range(2)], axis=1))
    deep[...] = exact_dot(jnp.concatenate(pieces, 0), depth_table(0, (ZC, ZF)))
    for i in range(6):
        lift_plane(deep, 24 * i, lifted, i)

    for copy in copies:
        copy.wait()
    emits = []
    for side, message in ((0, x_lo), (1, x_hi)):
        fill_fine(slabs[side], (y_up, y_dn), None, (NF - WIDE) * side, WIDE)
        slabs[side].halo_end(0, lambda k, t, message=message: message[fine_place(k, t)], True)

        def emit(x, own, side=side):
            at = 6 - x if side else x - 3
            low, high = 3 * side + lax.div(at, 2), 3 * side + lax.div(at + 1, 2)
            edge[side, at] = own + lifted_plane(lifted, low, high)

        emits.append(emit)
    smooth(slabs, 3, 10, lambda k: k, lambda k: 10 - k, emits)

    restrict_plane(slabs[0], 0, WIDE, 1, grown, mixed, 0)
    restrict_plane(slabs[1], 6, 5, 7, grown, mixed, NC)
    result = exact_dot(mixed[...], 0.5 * depth_table(1, (ZF, ZC)))
    finish = []
    for side in range(2):
        edge_r[side, 0] = result[NC * side : NC * (side + 1)]
        pairs = ((edge, out, 4, NF), (edge_r, out_r, 1, NC))
        for a, (source, target, size, length) in enumerate(pairs):
            finish.append(
                pltpu.make_async_copy(
                    source.at[side],
                    target.at[pl.ds((length - size) * side, size)],
                    out_sems.at[2 * side + a],
                )
            )
    for copy in finish:
        copy.start()
    for copy in finish:
        copy.wait()


def outer(u, c, f, e, cc, cs, y_up, y_dn, x_lo, x_hi, mid, mid_r):
    anywhere = pl.BlockSpec(memory_space=pl.ANY)
    vmem = pl.BlockSpec(memory_space=pltpu.VMEM)
    return pl.pallas_call(
        outer_kernel,
        in_specs=[anywhere] * 3 + [vmem] * 7 + [anywhere] * 2,
        out_specs=[anywhere, anywhere, vmem],
        out_shape=[
            jax.ShapeDtypeStruct((NF, NF, ZF), F32),
            jax.ShapeDtypeStruct((NC, NC, ZC), F32),
            jax.ShapeDtypeStruct((NC, NC, ZC), F32),
        ],
        scratch_shapes=[
            pltpu.SemaphoreType.DMA((2, 3, 4)),
            pltpu.SemaphoreType.DMA((4,)),
            pltpu.VMEM((4, NF + 8, 128), F32),
            pltpu.VMEM((2 * NC, ZF), F32),
            pltpu.VMEM((24 * 6, ZF), F32),
            pltpu.VMEM((6, 4, NF, 128), F32),
            pltpu.VMEM((2, 4, NF, ZF), F32),
            pltpu.VMEM((2, 1, NC, ZC), F32),
        ]
        + (Slab.natural(WIDE + 1, TF, ZF) + Slab.work(WIDE + 3, TF, ZF)) * 2
        + Slab.natural(NC + 1, TC, ZC)
        + Slab.work(NC + 6, TC, ZC),
        compiler_params=pltpu.CompilerParams(vmem_limit_bytes=LIMIT),
        input_output_aliases={10: 0, 11: 1},
        name="outer_planes",
    )(u, c, f, e, cc, cs, y_up, y_dn, x_lo, x_hi, mid, mid_r)


def shift(block, axis, by):
    count = lax.axis_size(axis)
    return lax.ppermute(block, axis, [(i, (i + by) % count) for i in range(count)])


def local(u, f, c, e, cs, cc):
    y_up, y_dn = pack_y(u, c, f, e, cc, cs)
    y_up = shift(y_up, "gy", -1)
    y_dn = shift(y_dn, "gy", 1)
    x_lo, x_hi = pack_x(u, c, f, e, cc, cs, y_up, y_dn)
    from_hi = shift(x_lo, "gx", -1)
    from_lo = shift(x_hi, "gx", 1)
    mid, mid_r = inner(u, c, f, e, y_up, y_dn)
    return tuple(outer(u, c, f, e, cc, cs, y_up, y_dn, from_lo, from_hi, mid, mid_r))


def solution(mesh):
    placed = P("gx", "gy", None)
    return jax.shard_map(
        local,
        mesh=mesh,
        in_specs=(placed,) * 6,
        out_specs=(placed,) * 3,
        check_vma=False,
    )
```

```python
import jax
import jax.numpy as jnp
from jax import lax
from jax.experimental import pallas as pl
from jax.experimental.pallas import tpu as pltpu
from jax.sharding import PartitionSpec as P

MASS = 0.2
THETA = 1.125
DELTA = 0.875
SIGMA = THETA / DELTA
STEPS = 4
F32 = jnp.float32

NF, ZF, TF = 32, 512, 5
NC, ZC, TC = 16, 256, 3
XROWS = 7 * 8 * TF + 4 * 8 * TC
YROWS = 8 * (NF + NF // 2 + 12)
LIMIT = 60 * 1024 * 1024
PACK_LIMIT = 16 * 1024 * 1024
INNER_LIMIT = 40 * 1024 * 1024
OUTER_LIMIT = 32 * 1024 * 1024


def step_factors():
    ratio = 1.0 / SIGMA
    factors = []
    for _ in range(STEPS - 1):
        following = 1.0 / (2.0 * SIGMA - ratio)
        factors.append((following * ratio, 2.0 * following / DELTA))
        ratio = following
    return factors


def upper_rows(shape):
    return lax.broadcasted_iota(jnp.int32, shape, len(shape) - 2) < 4


def turn(block):
    return pltpu.roll(block, 4, axis=block.ndim - 2)


def pair_up(first, second):
    return jnp.where(upper_rows(first.shape), first, turn(second))


def pair_down(first, second):
    return jnp.where(upper_rows(first.shape), turn(second), first)


def halo_first(up, down):
    return jnp.where(upper_rows(up.shape), up, down)


def halo_second(up, down):
    return turn(jnp.where(upper_rows(up.shape), down, up))


def pack_y_kernel(u_r0, u_r3, c_r0, c_r3, f_r0, f_r3, e, cc, cs, y_up, y_dn):
    for x in range(NF):
        y_up[8 * x : 8 * x + 8, :] = pair_up(u_r0[x], c_r0[x])
        y_dn[8 * x : 8 * x + 8, :] = pair_down(u_r3[x], c_r3[x])
    for m in range(NF // 2):
        row = 8 * (NF + m)
        y_up[row : row + 8, :] = pair_up(f_r0[2 * m], f_r0[2 * m + 1])
        y_dn[row : row + 8, :] = pair_down(f_r3[2 * m], f_r3[2 * m + 1])
    for h in range(NC + NC // 2):
        row = 8 * (NF + NF // 2 + h // 2)
        lanes = slice(ZC * (h % 2), ZC * (h % 2 + 1))
        if h < NC:
            pair = ((e, h), (cc, h))
        else:
            pair = ((cs, 2 * (h - NC)), (cs, 2 * (h - NC) + 1))
        low = [ref[i, 0:8, :] for ref, i in pair]
        high = [ref[i, 8:16, :] for ref, i in pair]
        y_up[row : row + 8, lanes] = pair_up(*low)
        y_dn[row : row + 8, lanes] = pair_down(*high)


def pack_y(u, c, f, e, cc, cs):
    def strip(at):
        return pl.BlockSpec((NF, 8, ZF), lambda i: (0, at, 0))

    whole = pl.BlockSpec((NC, NC, ZC), lambda i: (0, 0, 0))
    y_spec = pl.BlockSpec((YROWS, ZF), lambda i: (0, 0))
    return pl.pallas_call(
        pack_y_kernel,
        grid=(1,),
        in_specs=[strip(0), strip(3)] * 3 + [whole] * 3,
        out_specs=[y_spec, y_spec],
        out_shape=[jax.ShapeDtypeStruct((YROWS, ZF), F32)] * 2,
        compiler_params=pltpu.CompilerParams(vmem_limit_bytes=LIMIT),
        name="pack_gy_faces",
    )(u, u, c, c, f, f, e, cc, cs)


class Slab:
    def __init__(self, own, tiles, depth, scale, natural, work, shift=0, flipped=False):
        self.own, self.t, self.z, self.scale = own, tiles, depth, scale
        self.lanes, self.shift, self.flipped = depth // 128, shift, flipped
        self.u, self.c, self.f = natural
        if work:
            (
                self.p, self.q, self.total, self.wx, self.wy, self.wz, self.wz_last,
                self.inv, self.flux, self.plane,
            ) = work

    @staticmethod
    def natural(planes, tiles, depth):
        return [pltpu.VMEM((planes, depth // 128, 8 * tiles, 128), F32)] * 3

    @staticmethod
    def work(planes, tiles, depth):
        rows, lanes = 8 * tiles, depth // 128
        return [pltpu.VMEM((planes, rows, depth), F32)] * 8 + [
            pltpu.VMEM((rows, depth), F32),
            pltpu.VMEM((lanes, rows, 128), F32),
        ]

    def at(self, x):
        return self.own - 1 - (x - self.shift) if self.flipped else x - self.shift

    def tile(self, ref, x, t):
        x = self.at(x)
        parts = [ref[x, j, pl.ds(t, 8, stride=self.t), :] for j in range(self.lanes)]
        return jnp.concatenate(parts, axis=1)

    def tiles(self, ref, x):
        return [self.tile(ref, x, t) for t in range(self.t)]

    def put_tile(self, ref, index, t, value):
        for j in range(self.lanes):
            ref[index, j, pl.ds(t, 8, stride=self.t), :] = value[:, 128 * j : 128 * (j + 1)]

    def rows(self, t):
        return slice(8 * t, 8 * t + 8)

    def put_halo(self, ref, index, block):
        top = 8 * (self.t - 1)
        for j in range(self.lanes):
            ref[index, j, top : top + 8, :] = block[:, 128 * j : 128 * (j + 1)]

    def put_own(self, ref, index, block):
        own = 8 * (self.t - 1)
        for j in range(self.lanes):
            ref[index, j, 0:own, :] = block[:, 128 * j : 128 * (j + 1)]

    def next_row(self, values):
        return values[1:] + [pltpu.roll(values[0], 7, axis=0)]

    def last_row(self, values):
        return [pltpu.roll(values[-1], 1, axis=0)] + values[:-1]

    def next_deep(self, value):
        return pltpu.roll(value, self.z - 1, axis=1)

    def last_deep(self, value):
        return pltpu.roll(value, 1, axis=1)

    def cross_weights(self, c):
        half = 0.5 * self.scale
        ahead, behind = self.next_row(c), self.last_row(c)
        wy = [half * (c[t] + ahead[t]) for t in range(self.t)]
        wy_last = [half * (c[0] + behind[0])] + wy[:-1]
        wz = [half * (v + self.next_deep(v)) for v in c]
        wz_last = [half * (v + self.last_deep(v)) for v in c]
        return wy, wy_last, wz, wz_last

    def cross_flow(self, v, wy, wy_last, wz, wz_last):
        ahead, behind = self.next_row(v), self.last_row(v)
        fy = [wy[t] * (ahead[t] - v[t]) for t in range(self.t)]
        fy_last = [wy_last[0] * (v[0] - behind[0])] + fy[:-1]
        flow = []
        for t in range(self.t):
            fz = wz[t] * (self.next_deep(v[t]) - v[t])
            fz_last = wz_last[t] * (v[t] - self.last_deep(v[t]))
            flow.append((fy[t] - fy_last[t]) + (fz - fz_last))
        return flow

    def keep_weights(self, x, t, wy, wz, wz_last, faces):
        rows = self.rows(t)
        inv = 1.0 / (MASS + faces)
        self.wy[x, rows, :] = wy
        self.wz[x, rows, :] = wz
        self.wz_last[x, rows, :] = wz_last
        self.inv[x, rows, :] = inv
        return inv

    def open_end(self, x):
        u0, u1 = self.tiles(self.u, x), self.tiles(self.u, x + 1)
        c0, c1 = self.tiles(self.c, x), self.tiles(self.c, x + 1)
        for t in range(self.t):
            w = 0.5 * self.scale * (c0[t] + c1[t])
            self.wx[x, self.rows(t), :] = w
            self.flux[self.rows(t), :] = w * (u1[t] - u0[t])

    def halo_end(self, far, read, start):
        half = 0.5 * self.scale
        step = 1 if start else -1
        mid, near, own = far + step, far + 2 * step, far + 3 * step
        message = [[read(k, t) for t in range(self.t)] for k in range(7)]
        u1, c1, c2, c3, r1, p2, p3 = message
        u_own, c_own = self.tiles(self.u, own), self.tiles(self.c, own)
        cross2, cross1 = self.cross_weights(c2), self.cross_weights(c1)
        for t in range(self.t):
            rows = self.rows(t)
            outer, middle, inner = half * (c3[t] + c2[t]), half * (c2[t] + c1[t]), half * (c1[t] + c_own[t])
            self.wx[min(far, mid), rows, :] = outer
            self.wx[min(mid, near), rows, :] = middle
            self.wx[min(near, own), rows, :] = inner
            self.p[far, rows, :] = p3[t]
            wy, wy_last, wz, wz_last = [w[t] for w in cross2]
            faces = (outer + middle) + (wy + wy_last) + (wz + wz_last)
            self.keep_weights(mid, t, wy, wz, wz_last, faces)
            self.p[mid, rows, :] = p2[t]
            self.q[mid, rows, :] = THETA * p2[t]
            wy, wy_last, wz, wz_last = [w[t] for w in cross1]
            faces = (middle + inner) + (wy + wy_last) + (wz + wz_last)
            inv = self.keep_weights(near, t, wy, wz, wz_last, faces)
            flux = inner * (u_own[t] - u1[t])
            residual = r1[t] + flux
            q = residual * inv
            self.q[near, rows, :] = q
            self.p[near, rows, :] = q * (1.0 / THETA)
            if start:
                self.flux[rows, :] = flux
                self.put_tile(self.f, self.own, t, residual)

    def first_plane(self, x, known=None, more=False):
        half = 0.5 * self.scale
        every = range(self.t)
        if known is None:
            u, c = self.tiles(self.u, x), self.tiles(self.c, x)
            fx_last = [self.flux[self.rows(t), :] for t in every]
            wx_last = [self.wx[x - 1, self.rows(t), :] for t in every]
        else:
            u, c, fx_last, wx_last = known
        u_next, c_next = self.tiles(self.u, x + 1), self.tiles(self.c, x + 1)
        kept_fx, kept_wx = [], []
        wy, wy_last, wz, wz_last = self.cross_weights(c)
        cross = self.cross_flow(u, wy, wy_last, wz, wz_last)
        for t in range(self.t):
            rows = self.rows(t)
            wx = half * (c[t] + c_next[t])
            fx = wx * (u_next[t] - u[t])
            faces = (wx + wx_last[t]) + (wy[t] + wy_last[t]) + (wz[t] + wz_last[t])
            inv = self.keep_weights(x, t, wy[t], wz[t], wz_last[t], faces)
            flow = (fx - fx_last[t]) + cross[t]
            residual = self.tile(self.f, x, t) - MASS * u[t] + flow
            q = residual * inv
            p = q * (1.0 / THETA)
            kept_fx.append(fx)
            kept_wx.append(wx)
            if not more:
                self.flux[rows, :] = fx
            self.wx[x, rows, :] = wx
            self.q[x, rows, :] = q
            self.p[x, rows, :] = p
            self.total[x, rows, :] = u[t] + p
            self.put_tile(self.f, self.at(x), t, residual)
        return u_next, c_next, kept_fx, kept_wx

    def start_step(self, x):
        for t in range(self.t):
            rows = self.rows(t)
            change = self.p[x, rows, :] - self.p[x - 1, rows, :]
            self.flux[rows, :] = self.wx[x - 1, rows, :] * change

    def step_plane(self, level, x, emit, known=None, more=False):
        keep, gain = step_factors()[level - 1]
        every = range(self.t)
        if known is None:
            p = [self.p[x, self.rows(t), :] for t in every]
            fx_last = [self.flux[self.rows(t), :] for t in every]
        else:
            p, fx_last = known
        p_next = [self.p[x + 1, self.rows(t), :] for t in every]
        kept = []
        weights = [
            [ref[x, self.rows(t), :] for t in range(self.t)]
            for ref in (self.wy, self.wz, self.wz_last)
        ]
        wy_last = self.last_row(weights[0])
        cross = self.cross_flow(p, weights[0], wy_last, weights[1], weights[2])
        for t in range(self.t):
            rows = self.rows(t)
            fx = self.wx[x, rows, :] * (p_next[t] - p[t])
            flow = (fx - fx_last[t]) + cross[t]
            kept.append(fx)
            if not more:
                self.flux[rows, :] = fx
            q = self.q[x, rows, :] + self.inv[x, rows, :] * (flow - MASS * p[t])
            new = keep * p[t] + gain * q
            total = self.total[x, rows, :] + new
            if emit is None:
                self.q[x, rows, :] = q
                self.p[x, rows, :] = new
                self.total[x, rows, :] = total
            else:
                for j in range(self.lanes):
                    at = pl.ds(t, 8, stride=self.t)
                    self.plane[j, at, :] = total[:, 128 * j : 128 * (j + 1)]
        if emit is not None:
            own = 8 * (self.t - 1)
            parts = [self.plane[j, 0:own, :] for j in range(self.lanes)]
            emit(x, jnp.concatenate(parts, axis=1))
        return p_next, kept


def sweep(slabs, low, high, act):
    if (high - low) % 2:
        for slab in slabs:
            act(slab, low, None, False)
        low += 1

    def body(i, carry):
        x = low + 2 * i
        known = [act(slab, x, None, True) for slab in slabs]
        for slab, value in zip(slabs, known):
            act(slab, x + 1, value, False)
        return carry

    lax.fori_loop(0, (high - low) // 2, body, 0)


def first_sweep(slabs, low, high):
    sweep(slabs, low, high, lambda slab, x, known, more: slab.first_plane(x, known, more))


def step_sweeps(slabs, low, high, emits):
    for level in range(1, STEPS):
        for slab in slabs:
            slab.start_step(low(level))

        def act(slab, x, known, more, level=level):
            emit = emits[slabs.index(slab)] if level == STEPS - 1 else None
            return slab.step_plane(level, x, emit, known, more)

        sweep(slabs, low(level), high(level), act)


def depth_table(coarse_axis, shape):
    fine_len = shape[1 - coarse_axis]
    fine = lax.broadcasted_iota(jnp.int32, shape, 1 - coarse_axis)
    coarse = lax.broadcasted_iota(jnp.int32, shape, coarse_axis)
    near = (fine == 2 * coarse + 1) | (fine == lax.rem(2 * coarse - 1 + fine_len, fine_len))
    return jnp.where(fine == 2 * coarse, 1.0, jnp.where(near, 0.5, 0.0))


def exact_dot(field, table):
    table = table.astype(jnp.bfloat16)
    head = field.astype(jnp.bfloat16)
    rest = field - head.astype(F32)
    middle = rest.astype(jnp.bfloat16)
    tail = (rest - middle.astype(F32)).astype(jnp.bfloat16)
    parts = [jnp.dot(v, table, preferred_element_type=F32) for v in (head, middle, tail)]
    return (parts[2] + parts[1]) + parts[0]


def restrict_plane(slab, at, before, after, grown, out_ref, row):
    for j in range(4):
        mixed = 0.5 * slab.f[at, j] + 0.25 * (slab.f[before, j] + slab.f[after, j])
        grown[j, 0:8, :] = mixed[NF : NF + 8]
        grown[j, 8 : 8 + NF, :] = mixed[0:NF]
        middle = grown[j, pl.ds(8, NC, stride=2), :]
        beside = grown[j, pl.ds(9, NC, stride=2), :] + grown[j, pl.ds(7, NC, stride=2), :]
        out_ref[pl.ds(row, NC), 128 * j : 128 * (j + 1)] = 0.5 * middle + 0.25 * beside


def lift_plane(deep, row, lifted, at):
    if not isinstance(row, int):
        row = pl.multiple_of(row, 8)
    block = deep[pl.ds(row, 24), :]
    here, there = block[0:NC], pltpu.roll(block, 23, axis=0)[0:NC]
    between = 0.5 * (here + there)
    for j in range(4):
        lanes = slice(128 * j, 128 * (j + 1))
        lifted[at, j, pl.ds(0, NC, stride=2), :] = here[:, lanes]
        lifted[at, j, pl.ds(1, NC, stride=2), :] = between[:, lanes]


def lifted_plane(lifted, low, high):
    parts = [0.5 * (lifted[low, j] + lifted[high, j]) for j in range(4)]
    return jnp.concatenate(parts, axis=1)


def coarse_halo(y_up, y_dn, base, h):
    row = base + 8 * (h // 2)
    lanes = slice(ZC * (h % 2), ZC * (h % 2 + 1))
    return y_up[row : row + 8, lanes], y_dn[row : row + 8, lanes]


def inner_kernel(u, c, f, e, y_up, y_dn, out, out_r, *scratch):
    sems, grown, mixed, deep, lifted = scratch[:5]
    slab = Slab(NF, TF, ZF, 1.0, scratch[5:8], scratch[8:])
    copies = []
    for m in range(4):
        for a, (source, target) in enumerate(((u, slab.u), (c, slab.c), (f, slab.f))):
            for j in range(4):
                copies.append(
                    pltpu.make_async_copy(
                        source.at[pl.ds(8 * m, 8), :, pl.ds(128 * j, 128)],
                        target.at[pl.ds(8 * m, 8), j, pl.ds(0, NF), :],
                        sems.at[m, a, j],
                    )
                )
    for copy in copies:
        copy.start()

    pieces = []
    for i in range(NC):
        up, down = coarse_halo(y_up, y_dn, 8 * (NF + NF // 2), i)
        pieces += [e[i], halo_first(up, down)]
    deep[...] = exact_dot(jnp.concatenate(pieces, 0), depth_table(0, (ZC, ZF)))

    def raise_one(i, carry):
        lift_plane(deep, 24 * i, lifted, i)
        return carry

    lax.fori_loop(2, NC - 1, raise_one, 0)
    def fill(m, carry):
        for half in range(2):
            x = 2 * m + half
            row = pl.multiple_of(8 * x, 8)
            up, down = y_up[pl.ds(row, 8), :], y_dn[pl.ds(row, 8), :]
            slab.put_halo(slab.u, x, halo_first(up, down))
            slab.put_halo(slab.c, x, halo_second(up, down))
        row = pl.multiple_of(8 * (NF + m), 8)
        up, down = y_up[pl.ds(row, 8), :], y_dn[pl.ds(row, 8), :]
        slab.put_halo(slab.f, 2 * m, halo_first(up, down))
        slab.put_halo(slab.f, 2 * m + 1, halo_second(up, down))
        return carry

    lax.fori_loop(0, NF // 2, fill, 0)

    def emit(x, own):
        out[x] = own + lifted_plane(lifted, lax.div(x, 2), lax.div(x + 1, 2))

    for m in range(4):
        for copy in copies[12 * m : 12 * (m + 1)]:
            copy.wait()
        if m == 0:
            slab.open_end(0)
        first_sweep([slab], max(8 * m - 1, 1), 8 * m + 7)
    step_sweeps([slab], lambda k: 1 + k, lambda k: NF - 1 - k, [emit])

    def lower(i, carry):
        row = pl.multiple_of(NC * (i - 1), 8)
        restrict_plane(slab, 2 * i, 2 * i - 1, 2 * i + 1, grown, mixed, row)
        return carry

    lax.fori_loop(1, NC - 1, lower, 0)
    result = exact_dot(mixed[...], 0.5 * depth_table(1, (ZF, ZC)))
    for i in range(1, NC - 1):
        out_r[i] = result[NC * (i - 1) : NC * i]


def inner(u, c, f, e, y_up, y_dn):
    anywhere = pl.BlockSpec(memory_space=pl.ANY)
    vmem = pl.BlockSpec(memory_space=pltpu.VMEM)
    return pl.pallas_call(
        inner_kernel,
        in_specs=[anywhere] * 3 + [vmem] * 3,
        out_specs=[vmem, vmem],
        out_shape=[
            jax.ShapeDtypeStruct((NF, NF, ZF), F32),
            jax.ShapeDtypeStruct((NC, NC, ZC), F32),
        ],
        scratch_shapes=[
            pltpu.SemaphoreType.DMA((4, 3, 4)),
            pltpu.VMEM((4, NF + 8, 128), F32),
            pltpu.VMEM((NC * (NC - 2), ZF), F32),
            pltpu.VMEM((24 * NC, ZF), F32),
            pltpu.VMEM((NC, 4, NF, 128), F32),
        ]
        + Slab.natural(NF, TF, ZF)
        + Slab.work(NF, TF, ZF),
        compiler_params=pltpu.CompilerParams(vmem_limit_bytes=INNER_LIMIT),
        cost_estimate=pl.CostEstimate(
            flops=30_000_000_000, bytes_accessed=12_000_000, transcendentals=0
        ),
        name="inner_planes",
    )(u, c, f, e, y_up, y_dn)


def first_planes(slab, write):
    half = 0.5 * slab.scale
    u, c = [[slab.tiles(ref, x) for x in range(4)] for ref in (slab.u, slab.c)]
    wx = [[half * (c[x][t] + c[x + 1][t]) for t in range(slab.t)] for x in range(3)]
    fx = [[wx[x][t] * (u[x + 1][t] - u[x][t]) for t in range(slab.t)] for x in range(3)]
    for t in range(slab.t):
        write(0, t, u[0][t])
        for x in range(3):
            write(1 + x, t, c[x][t])
    for x in range(3):
        weights = slab.cross_weights(c[x])
        cross = slab.cross_flow(u[x], *weights)
        for t in range(slab.t):
            part = slab.tile(slab.f, x, t) - MASS * u[x][t] + cross[t] + fx[x][t]
            if x == 0:
                write(4, t, part)
                continue
            wy, wy_last, wz, wz_last = [w[t] for w in weights]
            faces = (wx[x][t] + wx[x - 1][t]) + (wy + wy_last) + (wz + wz_last)
            write(4 + x, t, (part - fx[x - 1][t]) / (MASS + faces) * (1.0 / THETA))


def fine_place(k, t):
    row = 8 * TF * k + 8 * t
    return slice(row, row + 8), slice(0, ZF)


def coarse_place(k, t):
    row = 7 * 8 * TF + 8 * TC * (k // 2) + 8 * t
    return slice(row, row + 8), slice(ZC * (k % 2), ZC * (k % 2 + 1))


def fill_fine(slab, halo, blocks, first, planes):
    up, down, up_f, down_f = halo
    for i in range(planes):
        if blocks is not None:
            for target, block in zip((slab.u, slab.c, slab.f), blocks):
                slab.put_own(target, i, block[i])
        pair = (up[8 * i : 8 * i + 8, :], down[8 * i : 8 * i + 8, :])
        slab.put_halo(slab.u, i, halo_first(*pair))
        slab.put_halo(slab.c, i, halo_second(*pair))
        row = 8 * (i // 2)
        pair = (up_f[row : row + 8, :], down_f[row : row + 8, :])
        slab.put_halo(slab.f, i, (halo_second if i % 2 else halo_first)(*pair))


def fill_coarse(slab, refs, fields, planes):
    for x, place in planes:
        for target, source in zip((slab.u, slab.c, slab.f), fields):
            slab.put_own(target, place, source[x])
        pair = coarse_halo(*refs, 0, x)
        slab.put_halo(slab.u, place, halo_first(*pair))
        slab.put_halo(slab.c, place, halo_second(*pair))
        pair = coarse_halo(*refs, 0, NC + x // 2)
        slab.put_halo(slab.f, place, (halo_second if x % 2 else halo_first)(*pair))


def side_halos(planes):
    specs = []
    for side in range(2):
        at = (NF // planes - 1) * side
        for _ in range(2):
            specs.append(pl.BlockSpec((8 * planes, ZF), lambda i, at=at: (at, 0)))
        at += 2 * NF // planes
        for _ in range(2):
            specs.append(pl.BlockSpec((4 * planes, ZF), lambda i, at=at: (at, 0)))
    return specs


COARSE_HALO = pl.BlockSpec((8 * 12, ZF), lambda i: (4, 0))


def pack_x_kernel(u_lo, u_hi, c_lo, c_hi, f_lo, f_hi, e, cc, cs, *refs):
    halos, coarse_halos, outs = (refs[:4], refs[4:8]), refs[8:10], refs[10:12]
    scratch = refs[12:]
    for side, blocks in ((0, (u_lo, c_lo, f_lo)), (1, (u_hi, c_hi, f_hi))):
        out = outs[side]
        slab = Slab(4, TF, ZF, 1.0, scratch[6 * side : 6 * side + 3], (), 0, side == 1)
        fill_fine(slab, halos[side], blocks, 28 * side, 4)

        def write_fine(k, t, value, out=out):
            out[fine_place(k, t)] = value

        first_planes(slab, write_fine)
        slab = Slab(4, TC, ZC, 0.25, scratch[6 * side + 3 : 6 * side + 6], (), 0, side == 1)
        fill_coarse(slab, coarse_halos, (e, cc, cs), [(12 * side + i, i) for i in range(4)])

        def write_coarse(k, t, value, out=out):
            out[coarse_place(k, t)] = value

        first_planes(slab, write_coarse)
        for t in range(TC):
            out[coarse_place(7, t)] = jnp.zeros((8, ZC), F32)


def pack_x(u, c, f, e, cc, cs, y_up, y_dn):
    def face(side):
        return pl.BlockSpec((4, NF, ZF), lambda i: (7 * side, 0, 0))

    whole = pl.BlockSpec((NC, NC, ZC), lambda i: (0, 0, 0))
    x_spec = pl.BlockSpec((XROWS, ZF), lambda i: (0, 0))
    return pl.pallas_call(
        pack_x_kernel,
        grid=(1,),
        in_specs=[face(0), face(1)] * 3 + [whole] * 3 + side_halos(4) + [COARSE_HALO] * 2,
        out_specs=[x_spec, x_spec],
        out_shape=[jax.ShapeDtypeStruct((XROWS, ZF), F32)] * 2,
        scratch_shapes=(Slab.natural(4, TF, ZF) + Slab.natural(4, TC, ZC)) * 2,
        compiler_params=pltpu.CompilerParams(vmem_limit_bytes=PACK_LIMIT),
        name="pack_gx_faces",
    )(u, u, c, c, f, f, e, cc, cs, *[y_up, y_dn] * 5)


WIDE = 8


def outer_kernel(
    u, c, f, e, cc, cs, *refs,
):
    halos, coarse_halos, messages = (refs[:4], refs[4:8]), refs[8:10], refs[10:12]
    x_lo, x_hi = messages
    out, out_r, out_c = refs[14:17]
    scratch = refs[17:]
    sems, out_sems, grown, mixed, deep, lifted, edge, edge_r = scratch[:8]
    slabs = []
    for side in range(2):
        refs = scratch[8 + 13 * side : 21 + 13 * side]
        slabs.append(Slab(WIDE, TF, ZF, 1.0, refs[:3], refs[3:], 3, side == 1))
    coarse = Slab(NC, TC, ZC, 0.25, scratch[34:37], scratch[37:47], 3)
    copies = []
    for side in range(2):
        slab = slabs[side]
        for a, (source, target) in enumerate(((u, slab.u), (c, slab.c), (f, slab.f))):
            for j in range(4):
                copies.append(
                    pltpu.make_async_copy(
                        source.at[pl.ds((NF - WIDE) * side, WIDE), :, pl.ds(128 * j, 128)],
                        target.at[pl.ds(0, WIDE), j, pl.ds(0, NF), :],
                        sems.at[side, a, j],
                    )
                )
    for copy in copies:
        copy.start()

    fill_coarse(coarse, coarse_halos, (e, cc, cs), [(x, x) for x in range(NC)])
    for t in range(TC):
        coarse.put_tile(coarse.u, NC, t, x_hi[coarse_place(0, t)])
        coarse.put_tile(coarse.c, NC, t, x_hi[coarse_place(1, t)])
    coarse.halo_end(0, lambda k, t: x_lo[coarse_place(k, t)], True)
    first_sweep([coarse], 3, 3 + NC)
    coarse.halo_end(5 + NC, lambda k, t: x_hi[coarse_place(k, t)], False)

    def emit_coarse(x, own):
        out_c[x - 3] = own

    step_sweeps([coarse], lambda k: k, lambda k: 6 + NC - k, [emit_coarse])

    pieces = []
    for x in (0, 1, 2, 14, 15, 16):
        pieces.append(jnp.concatenate([coarse.u[x, j] for j in range(2)], axis=1))
    deep[...] = exact_dot(jnp.concatenate(pieces, 0), depth_table(0, (ZC, ZF)))
    for i in range(6):
        lift_plane(deep, 24 * i, lifted, i)

    for copy in copies:
        copy.wait()
    emits = []
    for side, message in enumerate(messages):
        fill_fine(slabs[side], halos[side], None, (NF - WIDE) * side, WIDE)
        slabs[side].halo_end(0, lambda k, t, message=message: message[fine_place(k, t)], True)

        def emit(x, own, side=side):
            at = 6 - x if side else x - 3
            low, high = 3 * side + lax.div(at, 2), 3 * side + lax.div(at + 1, 2)
            edge[side, at] = own + lifted_plane(lifted, low, high)

        emits.append(emit)
    first_sweep(slabs, 3, 10)
    step_sweeps(slabs, lambda k: k, lambda k: 10 - k, emits)

    restrict_plane(slabs[0], 0, WIDE, 1, grown, mixed, 0)
    restrict_plane(slabs[1], 6, 5, 7, grown, mixed, NC)
    result = exact_dot(mixed[...], 0.5 * depth_table(1, (ZF, ZC)))
    finish = []
    for side in range(2):
        edge_r[side, 0] = result[NC * side : NC * (side + 1)]
        pairs = ((edge, out, 4, NF), (edge_r, out_r, 1, NC))
        for a, (source, target, size, length) in enumerate(pairs):
            finish.append(
                pltpu.make_async_copy(
                    source.at[side],
                    target.at[pl.ds((length - size) * side, size)],
                    out_sems.at[2 * side + a],
                )
            )
    for copy in finish:
        copy.start()
    for copy in finish:
        copy.wait()


def outer(u, c, f, e, cc, cs, y_up, y_dn, x_lo, x_hi, mid, mid_r):
    anywhere = pl.BlockSpec(memory_space=pl.ANY)
    whole = pl.BlockSpec((NC, NC, ZC), lambda i: (0, 0, 0))
    x_spec = pl.BlockSpec((XROWS, ZF), lambda i: (0, 0))
    halo_specs = side_halos(WIDE) + [COARSE_HALO] * 2
    return pl.pallas_call(
        outer_kernel,
        grid=(1,),
        in_specs=[anywhere] * 3 + [whole] * 3 + halo_specs + [x_spec] * 2 + [anywhere] * 2,
        out_specs=[anywhere, anywhere, whole],
        out_shape=[
            jax.ShapeDtypeStruct((NF, NF, ZF), F32),
            jax.ShapeDtypeStruct((NC, NC, ZC), F32),
            jax.ShapeDtypeStruct((NC, NC, ZC), F32),
        ],
        scratch_shapes=[
            pltpu.SemaphoreType.DMA((2, 3, 4)),
            pltpu.SemaphoreType.DMA((4,)),
            pltpu.VMEM((4, NF + 8, 128), F32),
            pltpu.VMEM((2 * NC, ZF), F32),
            pltpu.VMEM((24 * 6, ZF), F32),
            pltpu.VMEM((6, 4, NF, 128), F32),
            pltpu.VMEM((2, 4, NF, ZF), F32),
            pltpu.VMEM((2, 1, NC, ZC), F32),
        ]
        + (Slab.natural(WIDE + 1, TF, ZF) + Slab.work(WIDE + 3, TF, ZF)) * 2
        + Slab.natural(NC + 1, TC, ZC)
        + Slab.work(NC + 6, TC, ZC),
        compiler_params=pltpu.CompilerParams(vmem_limit_bytes=OUTER_LIMIT),
        input_output_aliases={18: 0, 19: 1},
        name="outer_planes",
    )(u, c, f, e, cc, cs, *[y_up, y_dn] * 5, x_lo, x_hi, mid, mid_r)


def shift(block, axis, by):
    count = lax.axis_size(axis)
    return lax.ppermute(block, axis, [(i, (i + by) % count) for i in range(count)])


def local(u, f, c, e, cs, cc):
    y_up, y_dn = pack_y(u, c, f, e, cc, cs)
    y_up = shift(y_up, "gy", -1)
    y_dn = shift(y_dn, "gy", 1)
    x_lo, x_hi = pack_x(u, c, f, e, cc, cs, y_up, y_dn)
    from_hi = shift(x_lo, "gx", -1)
    from_lo = shift(x_hi, "gx", 1)
    mid, mid_r = inner(u, c, f, e, y_up, y_dn)
    return tuple(outer(u, c, f, e, cc, cs, y_up, y_dn, from_lo, from_hi, mid, mid_r))


def solution(mesh):
    placed = P("gx", "gy", None)
    return jax.shard_map(
        local,
        mesh=mesh,
        in_specs=(placed,) * 6,
        out_specs=(placed,) * 3,
        check_vma=False,
    )
```

```python
import jax
import jax.numpy as jnp
from jax import lax
from jax.experimental import pallas as pl
from jax.experimental.pallas import tpu as pltpu
from jax.sharding import PartitionSpec as P

MASS = 0.2
THETA = 1.125
DELTA = 0.875
SIGMA = THETA / DELTA
STEPS = 4
F32 = jnp.float32

NF, ZF, TF = 32, 512, 5
NC, ZC, TC = 16, 256, 3
XROWS = 7 * 8 * TF + 4 * 8 * TC
YROWS = 8 * (NF + NF // 2 + 12)
LIMIT = 60 * 1024 * 1024
PACK_LIMIT = 16 * 1024 * 1024
INNER_LIMIT = 40 * 1024 * 1024
OUTER_LIMIT = 32 * 1024 * 1024


def step_factors():
    ratio = 1.0 / SIGMA
    factors = []
    for _ in range(STEPS - 1):
        following = 1.0 / (2.0 * SIGMA - ratio)
        factors.append((following * ratio, 2.0 * following / DELTA))
        ratio = following
    return factors


def upper_rows(shape):
    return lax.broadcasted_iota(jnp.int32, shape, len(shape) - 2) < 4


def turn(block):
    return pltpu.roll(block, 4, axis=block.ndim - 2)


def pair_up(first, second):
    return jnp.where(upper_rows(first.shape), first, turn(second))


def pair_down(first, second):
    return jnp.where(upper_rows(first.shape), turn(second), first)


def halo_first(up, down):
    return jnp.where(upper_rows(up.shape), up, down)


def halo_second(up, down):
    return turn(jnp.where(upper_rows(up.shape), down, up))


def pack_y_kernel(u_r0, u_r3, c_r0, c_r3, f_r0, f_r3, e, cc, cs, y_up, y_dn):
    for x in range(NF):
        y_up[8 * x : 8 * x + 8, :] = pair_up(u_r0[x], c_r0[x])
        y_dn[8 * x : 8 * x + 8, :] = pair_down(u_r3[x], c_r3[x])
    for m in range(NF // 2):
        row = 8 * (NF + m)
        y_up[row : row + 8, :] = pair_up(f_r0[2 * m], f_r0[2 * m + 1])
        y_dn[row : row + 8, :] = pair_down(f_r3[2 * m], f_r3[2 * m + 1])
    for h in range(NC + NC // 2):
        row = 8 * (NF + NF // 2 + h // 2)
        lanes = slice(ZC * (h % 2), ZC * (h % 2 + 1))
        if h < NC:
            pair = ((e, h), (cc, h))
        else:
            pair = ((cs, 2 * (h - NC)), (cs, 2 * (h - NC) + 1))
        low = [ref[i, 0:8, :] for ref, i in pair]
        high = [ref[i, 8:16, :] for ref, i in pair]
        y_up[row : row + 8, lanes] = pair_up(*low)
        y_dn[row : row + 8, lanes] = pair_down(*high)


def pack_y(u, c, f, e, cc, cs):
    def strip(at):
        return pl.BlockSpec((NF, 8, ZF), lambda i: (0, at, 0))

    whole = pl.BlockSpec((NC, NC, ZC), lambda i: (0, 0, 0))
    y_spec = pl.BlockSpec((YROWS, ZF), lambda i: (0, 0))
    return pl.pallas_call(
        pack_y_kernel,
        grid=(1,),
        in_specs=[strip(0), strip(3)] * 3 + [whole] * 3,
        out_specs=[y_spec, y_spec],
        out_shape=[jax.ShapeDtypeStruct((YROWS, ZF), F32)] * 2,
        compiler_params=pltpu.CompilerParams(vmem_limit_bytes=LIMIT),
        name="pack_gy_faces",
    )(u, u, c, c, f, f, e, cc, cs)


class Slab:
    def __init__(self, own, tiles, depth, scale, natural, work, shift=0, flipped=False):
        self.own, self.t, self.z, self.scale = own, tiles, depth, scale
        self.lanes, self.shift, self.flipped = depth // 128, shift, flipped
        self.u, self.c, self.f = natural
        if work:
            (
                self.p, self.q, self.total, self.wx, self.wy, self.wz, self.wz_last,
                self.inv, self.flux, self.plane,
            ) = work

    @staticmethod
    def natural(planes, tiles, depth):
        return [pltpu.VMEM((planes, depth // 128, 8 * tiles, 128), F32)] * 3

    @staticmethod
    def work(planes, tiles, depth):
        rows, lanes = 8 * tiles, depth // 128
        return [pltpu.VMEM((planes, rows, depth), F32)] * 8 + [
            pltpu.VMEM((rows, depth), F32),
            pltpu.VMEM((lanes, rows, 128), F32),
        ]

    def at(self, x):
        return self.own - 1 - (x - self.shift) if self.flipped else x - self.shift

    def tile(self, ref, x, t):
        x = self.at(x)
        parts = [ref[x, j, pl.ds(t, 8, stride=self.t), :] for j in range(self.lanes)]
        return jnp.concatenate(parts, axis=1)

    def tiles(self, ref, x):
        return [self.tile(ref, x, t) for t in range(self.t)]

    def put_tile(self, ref, index, t, value):
        for j in range(self.lanes):
            ref[index, j, pl.ds(t, 8, stride=self.t), :] = value[:, 128 * j : 128 * (j + 1)]

    def rows(self, t):
        return slice(8 * t, 8 * t + 8)

    def put_halo(self, ref, index, block):
        top = 8 * (self.t - 1)
        for j in range(self.lanes):
            ref[index, j, top : top + 8, :] = block[:, 128 * j : 128 * (j + 1)]

    def put_own(self, ref, index, block):
        own = 8 * (self.t - 1)
        for j in range(self.lanes):
            ref[index, j, 0:own, :] = block[:, 128 * j : 128 * (j + 1)]

    def next_row(self, values):
        return values[1:] + [pltpu.roll(values[0], 7, axis=0)]

    def last_row(self, values):
        return [pltpu.roll(values[-1], 1, axis=0)] + values[:-1]

    def next_deep(self, value):
        return pltpu.roll(value, self.z - 1, axis=1)

    def last_deep(self, value):
        return pltpu.roll(value, 1, axis=1)

    def cross_weights(self, c):
        half = 0.5 * self.scale
        ahead, behind = self.next_row(c), self.last_row(c)
        wy = [half * (c[t] + ahead[t]) for t in range(self.t)]
        wy_last = [half * (c[0] + behind[0])] + wy[:-1]
        wz = [half * (v + self.next_deep(v)) for v in c]
        wz_last = [half * (v + self.last_deep(v)) for v in c]
        return wy, wy_last, wz, wz_last

    def cross_flow(self, v, wy, wy_last, wz, wz_last):
        ahead, behind = self.next_row(v), self.last_row(v)
        fy = [wy[t] * (ahead[t] - v[t]) for t in range(self.t)]
        fy_last = [wy_last[0] * (v[0] - behind[0])] + fy[:-1]
        flow = []
        for t in range(self.t):
            fz = wz[t] * (self.next_deep(v[t]) - v[t])
            fz_last = wz_last[t] * (v[t] - self.last_deep(v[t]))
            flow.append((fy[t] - fy_last[t]) + (fz - fz_last))
        return flow

    def keep_weights(self, x, t, wy, wz, wz_last, faces):
        rows = self.rows(t)
        inv = 1.0 / (MASS + faces)
        self.wy[x, rows, :] = wy
        self.wz[x, rows, :] = wz
        self.wz_last[x, rows, :] = wz_last
        self.inv[x, rows, :] = inv
        return inv

    def open_end(self, x):
        u0, u1 = self.tiles(self.u, x), self.tiles(self.u, x + 1)
        c0, c1 = self.tiles(self.c, x), self.tiles(self.c, x + 1)
        for t in range(self.t):
            w = 0.5 * self.scale * (c0[t] + c1[t])
            self.wx[x, self.rows(t), :] = w
            self.flux[self.rows(t), :] = w * (u1[t] - u0[t])

    def halo_end(self, far, read, start):
        half = 0.5 * self.scale
        step = 1 if start else -1
        mid, near, own = far + step, far + 2 * step, far + 3 * step
        message = [[read(k, t) for t in range(self.t)] for k in range(7)]
        u1, c1, c2, c3, r1, p2, p3 = message
        u_own, c_own = self.tiles(self.u, own), self.tiles(self.c, own)
        cross2, cross1 = self.cross_weights(c2), self.cross_weights(c1)
        for t in range(self.t):
            rows = self.rows(t)
            outer, middle, inner = half * (c3[t] + c2[t]), half * (c2[t] + c1[t]), half * (c1[t] + c_own[t])
            self.wx[min(far, mid), rows, :] = outer
            self.wx[min(mid, near), rows, :] = middle
            self.wx[min(near, own), rows, :] = inner
            self.p[far, rows, :] = p3[t]
            wy, wy_last, wz, wz_last = [w[t] for w in cross2]
            faces = (outer + middle) + (wy + wy_last) + (wz + wz_last)
            self.keep_weights(mid, t, wy, wz, wz_last, faces)
            self.p[mid, rows, :] = p2[t]
            self.q[mid, rows, :] = THETA * p2[t]
            wy, wy_last, wz, wz_last = [w[t] for w in cross1]
            faces = (middle + inner) + (wy + wy_last) + (wz + wz_last)
            inv = self.keep_weights(near, t, wy, wz, wz_last, faces)
            flux = inner * (u_own[t] - u1[t])
            residual = r1[t] + flux
            q = residual * inv
            self.q[near, rows, :] = q
            self.p[near, rows, :] = q * (1.0 / THETA)
            if start:
                self.flux[rows, :] = flux
                self.put_tile(self.f, self.own, t, residual)

    def first_plane(self, x, known=None, more=False):
        half = 0.5 * self.scale
        every = range(self.t)
        if known is None:
            u, c = self.tiles(self.u, x), self.tiles(self.c, x)
            fx_last = [self.flux[self.rows(t), :] for t in every]
            wx_last = [self.wx[x - 1, self.rows(t), :] for t in every]
        else:
            u, c, fx_last, wx_last = known
        u_next, c_next = self.tiles(self.u, x + 1), self.tiles(self.c, x + 1)
        kept_fx, kept_wx = [], []
        wy, wy_last, wz, wz_last = self.cross_weights(c)
        cross = self.cross_flow(u, wy, wy_last, wz, wz_last)
        for t in range(self.t):
            rows = self.rows(t)
            wx = half * (c[t] + c_next[t])
            fx = wx * (u_next[t] - u[t])
            faces = (wx + wx_last[t]) + (wy[t] + wy_last[t]) + (wz[t] + wz_last[t])
            inv = self.keep_weights(x, t, wy[t], wz[t], wz_last[t], faces)
            flow = (fx - fx_last[t]) + cross[t]
            residual = self.tile(self.f, x, t) - MASS * u[t] + flow
            q = residual * inv
            p = q * (1.0 / THETA)
            kept_fx.append(fx)
            kept_wx.append(wx)
            if not more:
                self.flux[rows, :] = fx
            self.wx[x, rows, :] = wx
            self.q[x, rows, :] = q
            self.p[x, rows, :] = p
            self.total[x, rows, :] = u[t] + p
            self.put_tile(self.f, self.at(x), t, residual)
        return u_next, c_next, kept_fx, kept_wx

    def start_step(self, x):
        for t in range(self.t):
            rows = self.rows(t)
            change = self.p[x, rows, :] - self.p[x - 1, rows, :]
            self.flux[rows, :] = self.wx[x - 1, rows, :] * change

    def step_plane(self, level, x, emit, known=None, more=False):
        keep, gain = step_factors()[level - 1]
        every = range(self.t)
        if known is None:
            p = [self.p[x, self.rows(t), :] for t in every]
            fx_last = [self.flux[self.rows(t), :] for t in every]
        else:
            p, fx_last = known
        p_next = [self.p[x + 1, self.rows(t), :] for t in every]
        kept = []
        weights = [
            [ref[x, self.rows(t), :] for t in range(self.t)]
            for ref in (self.wy, self.wz, self.wz_last)
        ]
        wy_last = self.last_row(weights[0])
        cross = self.cross_flow(p, weights[0], wy_last, weights[1], weights[2])
        for t in range(self.t):
            rows = self.rows(t)
            fx = self.wx[x, rows, :] * (p_next[t] - p[t])
            flow = (fx - fx_last[t]) + cross[t]
            kept.append(fx)
            if not more:
                self.flux[rows, :] = fx
            q = self.q[x, rows, :] + self.inv[x, rows, :] * (flow - MASS * p[t])
            new = keep * p[t] + gain * q
            total = self.total[x, rows, :] + new
            if emit is None:
                self.q[x, rows, :] = q
                self.p[x, rows, :] = new
                self.total[x, rows, :] = total
            else:
                for j in range(self.lanes):
                    at = pl.ds(t, 8, stride=self.t)
                    self.plane[j, at, :] = total[:, 128 * j : 128 * (j + 1)]
        if emit is not None:
            own = 8 * (self.t - 1)
            parts = [self.plane[j, 0:own, :] for j in range(self.lanes)]
            emit(x, jnp.concatenate(parts, axis=1))
        return p_next, kept


def sweep(slabs, low, high, act):
    if (high - low) % 2:
        for slab in slabs:
            act(slab, low, None, False)
        low += 1

    def body(i, carry):
        x = low + 2 * i
        known = [act(slab, x, None, True) for slab in slabs]
        for slab, value in zip(slabs, known):
            act(slab, x + 1, value, False)
        return carry

    lax.fori_loop(0, (high - low) // 2, body, 0, unroll=2)


def first_sweep(slabs, low, high):
    sweep(slabs, low, high, lambda slab, x, known, more: slab.first_plane(x, known, more))


def step_sweeps(slabs, low, high, emits):
    for level in range(1, STEPS):
        for slab in slabs:
            slab.start_step(low(level))

        def act(slab, x, known, more, level=level):
            emit = emits[slabs.index(slab)] if level == STEPS - 1 else None
            return slab.step_plane(level, x, emit, known, more)

        sweep(slabs, low(level), high(level), act)


def depth_table(coarse_axis, shape):
    fine_len = shape[1 - coarse_axis]
    fine = lax.broadcasted_iota(jnp.int32, shape, 1 - coarse_axis)
    coarse = lax.broadcasted_iota(jnp.int32, shape, coarse_axis)
    near = (fine == 2 * coarse + 1) | (fine == lax.rem(2 * coarse - 1 + fine_len, fine_len))
    return jnp.where(fine == 2 * coarse, 1.0, jnp.where(near, 0.5, 0.0))


def exact_dot(field, table):
    table = table.astype(jnp.bfloat16)
    head = field.astype(jnp.bfloat16)
    rest = field - head.astype(F32)
    middle = rest.astype(jnp.bfloat16)
    tail = (rest - middle.astype(F32)).astype(jnp.bfloat16)
    parts = [jnp.dot(v, table, preferred_element_type=F32) for v in (head, middle, tail)]
    return (parts[2] + parts[1]) + parts[0]


def restrict_plane(slab, at, before, after, grown, out_ref, row):
    for j in range(4):
        mixed = 0.5 * slab.f[at, j] + 0.25 * (slab.f[before, j] + slab.f[after, j])
        grown[j, 0:8, :] = mixed[NF : NF + 8]
        grown[j, 8 : 8 + NF, :] = mixed[0:NF]
        middle = grown[j, pl.ds(8, NC, stride=2), :]
        beside = grown[j, pl.ds(9, NC, stride=2), :] + grown[j, pl.ds(7, NC, stride=2), :]
        out_ref[pl.ds(row, NC), 128 * j : 128 * (j + 1)] = 0.5 * middle + 0.25 * beside


def lift_plane(deep, row, lifted, at):
    if not isinstance(row, int):
        row = pl.multiple_of(row, 8)
    block = deep[pl.ds(row, 24), :]
    here, there = block[0:NC], pltpu.roll(block, 23, axis=0)[0:NC]
    between = 0.5 * (here + there)
    for j in range(4):
        lanes = slice(128 * j, 128 * (j + 1))
        lifted[at, j, pl.ds(0, NC, stride=2), :] = here[:, lanes]
        lifted[at, j, pl.ds(1, NC, stride=2), :] = between[:, lanes]


def lifted_plane(lifted, low, high):
    parts = [0.5 * (lifted[low, j] + lifted[high, j]) for j in range(4)]
    return jnp.concatenate(parts, axis=1)


def coarse_halo(y_up, y_dn, base, h):
    row = base + 8 * (h // 2)
    lanes = slice(ZC * (h % 2), ZC * (h % 2 + 1))
    return y_up[row : row + 8, lanes], y_dn[row : row + 8, lanes]


def inner_kernel(u, c, f, e, y_up, y_dn, out, out_r, *scratch):
    sems, grown, mixed, deep, lifted = scratch[:5]
    slab = Slab(NF, TF, ZF, 1.0, scratch[5:8], scratch[8:])
    copies = []
    for m in range(4):
        for a, (source, target) in enumerate(((u, slab.u), (c, slab.c), (f, slab.f))):
            for j in range(4):
                copies.append(
                    pltpu.make_async_copy(
                        source.at[pl.ds(8 * m, 8), :, pl.ds(128 * j, 128)],
                        target.at[pl.ds(8 * m, 8), j, pl.ds(0, NF), :],
                        sems.at[m, a, j],
                    )
                )
    for copy in copies:
        copy.start()

    pieces = []
    for i in range(NC):
        up, down = coarse_halo(y_up, y_dn, 8 * (NF + NF // 2), i)
        pieces += [e[i], halo_first(up, down)]
    deep[...] = exact_dot(jnp.concatenate(pieces, 0), depth_table(0, (ZC, ZF)))

    def raise_one(i, carry):
        lift_plane(deep, 24 * i, lifted, i)
        return carry

    lax.fori_loop(2, NC - 1, raise_one, 0)
    def fill(m, carry):
        for half in range(2):
            x = 2 * m + half
            row = pl.multiple_of(8 * x, 8)
            up, down = y_up[pl.ds(row, 8), :], y_dn[pl.ds(row, 8), :]
            slab.put_halo(slab.u, x, halo_first(up, down))
            slab.put_halo(slab.c, x, halo_second(up, down))
        row = pl.multiple_of(8 * (NF + m), 8)
        up, down = y_up[pl.ds(row, 8), :], y_dn[pl.ds(row, 8), :]
        slab.put_halo(slab.f, 2 * m, halo_first(up, down))
        slab.put_halo(slab.f, 2 * m + 1, halo_second(up, down))
        return carry

    lax.fori_loop(0, NF // 2, fill, 0)

    def emit(x, own):
        out[x] = own + lifted_plane(lifted, lax.div(x, 2), lax.div(x + 1, 2))

    for m in range(4):
        for copy in copies[12 * m : 12 * (m + 1)]:
            copy.wait()
        if m == 0:
            slab.open_end(0)
        first_sweep([slab], max(8 * m - 1, 1), 8 * m + 7)
    step_sweeps([slab], lambda k: 1 + k, lambda k: NF - 1 - k, [emit])

    def lower(i, carry):
        row = pl.multiple_of(NC * (i - 1), 8)
        restrict_plane(slab, 2 * i, 2 * i - 1, 2 * i + 1, grown, mixed, row)
        return carry

    lax.fori_loop(1, NC - 1, lower, 0)
    result = exact_dot(mixed[...], 0.5 * depth_table(1, (ZF, ZC)))
    for i in range(1, NC - 1):
        out_r[i] = result[NC * (i - 1) : NC * i]


def inner(u, c, f, e, y_up, y_dn):
    anywhere = pl.BlockSpec(memory_space=pl.ANY)
    vmem = pl.BlockSpec(memory_space=pltpu.VMEM)
    return pl.pallas_call(
        inner_kernel,
        in_specs=[anywhere] * 3 + [vmem] * 3,
        out_specs=[vmem, vmem],
        out_shape=[
            jax.ShapeDtypeStruct((NF, NF, ZF), F32),
            jax.ShapeDtypeStruct((NC, NC, ZC), F32),
        ],
        scratch_shapes=[
            pltpu.SemaphoreType.DMA((4, 3, 4)),
            pltpu.VMEM((4, NF + 8, 128), F32),
            pltpu.VMEM((NC * (NC - 2), ZF), F32),
            pltpu.VMEM((24 * NC, ZF), F32),
            pltpu.VMEM((NC, 4, NF, 128), F32),
        ]
        + Slab.natural(NF, TF, ZF)
        + Slab.work(NF, TF, ZF),
        compiler_params=pltpu.CompilerParams(vmem_limit_bytes=INNER_LIMIT),
        cost_estimate=pl.CostEstimate(
            flops=30_000_000_000, bytes_accessed=12_000_000, transcendentals=0
        ),
        name="inner_planes",
    )(u, c, f, e, y_up, y_dn)


def first_planes(slab, write):
    half = 0.5 * slab.scale
    u, c = [[slab.tiles(ref, x) for x in range(4)] for ref in (slab.u, slab.c)]
    wx = [[half * (c[x][t] + c[x + 1][t]) for t in range(slab.t)] for x in range(3)]
    fx = [[wx[x][t] * (u[x + 1][t] - u[x][t]) for t in range(slab.t)] for x in range(3)]
    for t in range(slab.t):
        write(0, t, u[0][t])
        for x in range(3):
            write(1 + x, t, c[x][t])
    for x in range(3):
        weights = slab.cross_weights(c[x])
        cross = slab.cross_flow(u[x], *weights)
        for t in range(slab.t):
            part = slab.tile(slab.f, x, t) - MASS * u[x][t] + cross[t] + fx[x][t]
            if x == 0:
                write(4, t, part)
                continue
            wy, wy_last, wz, wz_last = [w[t] for w in weights]
            faces = (wx[x][t] + wx[x - 1][t]) + (wy + wy_last) + (wz + wz_last)
            write(4 + x, t, (part - fx[x - 1][t]) / (MASS + faces) * (1.0 / THETA))


def fine_place(k, t):
    row = 8 * TF * k + 8 * t
    return slice(row, row + 8), slice(0, ZF)


def coarse_place(k, t):
    row = 7 * 8 * TF + 8 * TC * (k // 2) + 8 * t
    return slice(row, row + 8), slice(ZC * (k % 2), ZC * (k % 2 + 1))


def fill_fine(slab, halo, blocks, first, planes):
    up, down, up_f, down_f = halo
    for i in range(planes):
        if blocks is not None:
            for target, block in zip((slab.u, slab.c, slab.f), blocks):
                slab.put_own(target, i, block[i])
        pair = (up[8 * i : 8 * i + 8, :], down[8 * i : 8 * i + 8, :])
        slab.put_halo(slab.u, i, halo_first(*pair))
        slab.put_halo(slab.c, i, halo_second(*pair))
        row = 8 * (i // 2)
        pair = (up_f[row : row + 8, :], down_f[row : row + 8, :])
        slab.put_halo(slab.f, i, (halo_second if i % 2 else halo_first)(*pair))


def fill_coarse(slab, refs, fields, planes):
    for x, place in planes:
        for target, source in zip((slab.u, slab.c, slab.f), fields):
            slab.put_own(target, place, source[x])
        pair = coarse_halo(*refs, 0, x)
        slab.put_halo(slab.u, place, halo_first(*pair))
        slab.put_halo(slab.c, place, halo_second(*pair))
        pair = coarse_halo(*refs, 0, NC + x // 2)
        slab.put_halo(slab.f, place, (halo_second if x % 2 else halo_first)(*pair))


def side_halos(planes):
    specs = []
    for side in range(2):
        at = (NF // planes - 1) * side
        for _ in range(2):
            specs.append(pl.BlockSpec((8 * planes, ZF), lambda i, at=at: (at, 0)))
        at += 2 * NF // planes
        for _ in range(2):
            specs.append(pl.BlockSpec((4 * planes, ZF), lambda i, at=at: (at, 0)))
    return specs


COARSE_HALO = pl.BlockSpec((8 * 12, ZF), lambda i: (4, 0))


def pack_x_kernel(u_lo, u_hi, c_lo, c_hi, f_lo, f_hi, e, cc, cs, *refs):
    halos, coarse_halos, outs = (refs[:4], refs[4:8]), refs[8:10], refs[10:12]
    scratch = refs[12:]
    for side, blocks in ((0, (u_lo, c_lo, f_lo)), (1, (u_hi, c_hi, f_hi))):
        out = outs[side]
        slab = Slab(4, TF, ZF, 1.0, scratch[6 * side : 6 * side + 3], (), 0, side == 1)
        fill_fine(slab, halos[side], blocks, 28 * side, 4)

        def write_fine(k, t, value, out=out):
            out[fine_place(k, t)] = value

        first_planes(slab, write_fine)
        slab = Slab(4, TC, ZC, 0.25, scratch[6 * side + 3 : 6 * side + 6], (), 0, side == 1)
        fill_coarse(slab, coarse_halos, (e, cc, cs), [(12 * side + i, i) for i in range(4)])

        def write_coarse(k, t, value, out=out):
            out[coarse_place(k, t)] = value

        first_planes(slab, write_coarse)
        for t in range(TC):
            out[coarse_place(7, t)] = jnp.zeros((8, ZC), F32)


def pack_x(u, c, f, e, cc, cs, y_up, y_dn):
    def face(side):
        return pl.BlockSpec((4, NF, ZF), lambda i: (7 * side, 0, 0))

    whole = pl.BlockSpec((NC, NC, ZC), lambda i: (0, 0, 0))
    x_spec = pl.BlockSpec((XROWS, ZF), lambda i: (0, 0))
    return pl.pallas_call(
        pack_x_kernel,
        grid=(1,),
        in_specs=[face(0), face(1)] * 3 + [whole] * 3 + side_halos(4) + [COARSE_HALO] * 2,
        out_specs=[x_spec, x_spec],
        out_shape=[jax.ShapeDtypeStruct((XROWS, ZF), F32)] * 2,
        scratch_shapes=(Slab.natural(4, TF, ZF) + Slab.natural(4, TC, ZC)) * 2,
        compiler_params=pltpu.CompilerParams(vmem_limit_bytes=PACK_LIMIT),
        name="pack_gx_faces",
    )(u, u, c, c, f, f, e, cc, cs, *[y_up, y_dn] * 5)


WIDE = 8


def outer_kernel(
    u, c, f, e, cc, cs, *refs,
):
    halos, coarse_halos, messages = (refs[:4], refs[4:8]), refs[8:10], refs[10:12]
    x_lo, x_hi = messages
    out, out_r, out_c = refs[14:17]
    scratch = refs[17:]
    sems, out_sems, grown, mixed, deep, lifted, edge, edge_r = scratch[:8]
    slabs = []
    for side in range(2):
        refs = scratch[8 + 13 * side : 21 + 13 * side]
        slabs.append(Slab(WIDE, TF, ZF, 1.0, refs[:3], refs[3:], 3, side == 1))
    coarse = Slab(NC, TC, ZC, 0.25, scratch[34:37], scratch[37:47], 3)
    copies = []
    for side in range(2):
        slab = slabs[side]
        for a, (source, target) in enumerate(((u, slab.u), (c, slab.c), (f, slab.f))):
            for j in range(4):
                copies.append(
                    pltpu.make_async_copy(
                        source.at[pl.ds((NF - WIDE) * side, WIDE), :, pl.ds(128 * j, 128)],
                        target.at[pl.ds(0, WIDE), j, pl.ds(0, NF), :],
                        sems.at[side, a, j],
                    )
                )
    for copy in copies:
        copy.start()

    fill_coarse(coarse, coarse_halos, (e, cc, cs), [(x, x) for x in range(NC)])
    for t in range(TC):
        coarse.put_tile(coarse.u, NC, t, x_hi[coarse_place(0, t)])
        coarse.put_tile(coarse.c, NC, t, x_hi[coarse_place(1, t)])
    coarse.halo_end(0, lambda k, t: x_lo[coarse_place(k, t)], True)
    first_sweep([coarse], 3, 3 + NC)
    coarse.halo_end(5 + NC, lambda k, t: x_hi[coarse_place(k, t)], False)

    def emit_coarse(x, own):
        out_c[x - 3] = own

    step_sweeps([coarse], lambda k: k, lambda k: 6 + NC - k, [emit_coarse])

    pieces = []
    for x in (0, 1, 2, 14, 15, 16):
        pieces.append(jnp.concatenate([coarse.u[x, j] for j in range(2)], axis=1))
    deep[...] = exact_dot(jnp.concatenate(pieces, 0), depth_table(0, (ZC, ZF)))
    for i in range(6):
        lift_plane(deep, 24 * i, lifted, i)

    for copy in copies:
        copy.wait()
    emits = []
    for side, message in enumerate(messages):
        fill_fine(slabs[side], halos[side], None, (NF - WIDE) * side, WIDE)
        slabs[side].halo_end(0, lambda k, t, message=message: message[fine_place(k, t)], True)

        def emit(x, own, side=side):
            at = 6 - x if side else x - 3
            low, high = 3 * side + lax.div(at, 2), 3 * side + lax.div(at + 1, 2)
            edge[side, at] = own + lifted_plane(lifted, low, high)

        emits.append(emit)
    first_sweep(slabs, 3, 10)
    step_sweeps(slabs, lambda k: k, lambda k: 10 - k, emits)

    restrict_plane(slabs[0], 0, WIDE, 1, grown, mixed, 0)
    restrict_plane(slabs[1], 6, 5, 7, grown, mixed, NC)
    result = exact_dot(mixed[...], 0.5 * depth_table(1, (ZF, ZC)))
    finish = []
    for side in range(2):
        edge_r[side, 0] = result[NC * side : NC * (side + 1)]
        pairs = ((edge, out, 4, NF), (edge_r, out_r, 1, NC))
        for a, (source, target, size, length) in enumerate(pairs):
            finish.append(
                pltpu.make_async_copy(
                    source.at[side],
                    target.at[pl.ds((length - size) * side, size)],
                    out_sems.at[2 * side + a],
                )
            )
    for copy in finish:
        copy.start()
    for copy in finish:
        copy.wait()


def outer(u, c, f, e, cc, cs, y_up, y_dn, x_lo, x_hi, mid, mid_r):
    anywhere = pl.BlockSpec(memory_space=pl.ANY)
    whole = pl.BlockSpec((NC, NC, ZC), lambda i: (0, 0, 0))
    x_spec = pl.BlockSpec((XROWS, ZF), lambda i: (0, 0))
    halo_specs = side_halos(WIDE) + [COARSE_HALO] * 2
    return pl.pallas_call(
        outer_kernel,
        grid=(1,),
        in_specs=[anywhere] * 3 + [whole] * 3 + halo_specs + [x_spec] * 2 + [anywhere] * 2,
        out_specs=[anywhere, anywhere, whole],
        out_shape=[
            jax.ShapeDtypeStruct((NF, NF, ZF), F32),
            jax.ShapeDtypeStruct((NC, NC, ZC), F32),
            jax.ShapeDtypeStruct((NC, NC, ZC), F32),
        ],
        scratch_shapes=[
            pltpu.SemaphoreType.DMA((2, 3, 4)),
            pltpu.SemaphoreType.DMA((4,)),
            pltpu.VMEM((4, NF + 8, 128), F32),
            pltpu.VMEM((2 * NC, ZF), F32),
            pltpu.VMEM((24 * 6, ZF), F32),
            pltpu.VMEM((6, 4, NF, 128), F32),
            pltpu.VMEM((2, 4, NF, ZF), F32),
            pltpu.VMEM((2, 1, NC, ZC), F32),
        ]
        + (Slab.natural(WIDE + 1, TF, ZF) + Slab.work(WIDE + 3, TF, ZF)) * 2
        + Slab.natural(NC + 1, TC, ZC)
        + Slab.work(NC + 6, TC, ZC),
        compiler_params=pltpu.CompilerParams(vmem_limit_bytes=OUTER_LIMIT),
        input_output_aliases={18: 0, 19: 1},
        name="outer_planes",
    )(u, c, f, e, cc, cs, *[y_up, y_dn] * 5, x_lo, x_hi, mid, mid_r)


def shift(block, axis, by):
    count = lax.axis_size(axis)
    return lax.ppermute(block, axis, [(i, (i + by) % count) for i in range(count)])


def local(u, f, c, e, cs, cc):
    y_up, y_dn = pack_y(u, c, f, e, cc, cs)
    y_up = shift(y_up, "gy", -1)
    y_dn = shift(y_dn, "gy", 1)
    x_lo, x_hi = pack_x(u, c, f, e, cc, cs, y_up, y_dn)
    from_hi = shift(x_lo, "gx", -1)
    from_lo = shift(x_hi, "gx", 1)
    mid, mid_r = inner(u, c, f, e, y_up, y_dn)
    return tuple(outer(u, c, f, e, cc, cs, y_up, y_dn, from_lo, from_hi, mid, mid_r))


def solution(mesh):
    placed = P("gx", "gy", None)
    return jax.shard_map(
        local,
        mesh=mesh,
        in_specs=(placed,) * 6,
        out_specs=(placed,) * 3,
        check_vma=False,
    )
```
